512 devices in a mesh: dp: 64 (over z, x), tensor: 8 (over y, core).
Axes of the slice: x: 4, y: 4, z: 16, core: 2. Of those that a mesh axis runs over, the one named last changes fastest.
Arguments:
- x_slots: bfloat16 [640, 12288], P('dp', 'tensor'), may hold values from -6 to 6
- counts: int32 [64], replicated, may hold values from 1 to 10, 320 in all
- w_fc1: bfloat16 [24576, 12288], P('dp', 'tensor'), may hold values from -0.0546875 to 0.0546875
- b_fc1: float32 [24576], P('dp'), may hold values from -3 to 3
- upstream: bfloat16 [640, 24576], P('dp'), may hold values from -6 to 6
- owners: int32 [4096, 1], P('dp'), may hold values from 0 to 63; in each aligned block of 64 rows (0 to 63, 64 to 127, ...) at most 2 rows name the same one
Outputs:
- grad_slots: bfloat16 [640, 12288], P('dp', 'tensor')
- grad_bias: float32 [24576], P('dp')
- moved_grads: bfloat16 [8192, 6, 12288], P('dp', None, 'tensor')
The draws below stay inside these ranges and needn't reach their ends.
Inputs may be any that keep to these rules, and one draw needn't show every extreme that they name: Survivor s holds its counts[s] tokens in its first slots, in token order. `owners`: among the 64 blocks of one old owner (aligned rows), no new owner appears more than 2 times.
All inputs are finite; a program needn't handle non-finite values.
Results may differ from the reference program's by a relative error of at most 0.015.
Values may be sent and summed in bfloat16 or wider, within the bound.
No kernel may reach another device: no remote copies, remote signals or barrier semaphores. Data moves between devices by JAX's collectives and lax.ppermute only.
A program may use at most 64 MiB of HBM per device.

```python
import math
import jax
import jax.numpy as jnp
import numpy as np

D = 12288
FF = 24576
MOST = 2
SLOT_CAPACITY = 10
LOST_TOKENS = 320
GB = 64
BR = 6
N_DP = 64


def levels(rng, dims, split, smallest, largest):
    factor_of, own = 1.0, jax.random.fold_in(rng, 6)
    for dim, parts in split:
        heights = jnp.exp(jax.random.uniform(jax.random.fold_in(own, dim), (parts,), jnp.float32, smallest / len(split), largest / len(split)))
        factor_of = factor_of * jnp.repeat(heights, dims[dim] // parts).reshape([-1 if axis == dim else 1 for axis in range(len(dims))])
    return factor_of


def length_profile(count, total, reach, slope):
    loads = [(1 << 20) // math.isqrt(standing ** slope) + 1 for standing in range(2, count + 1)]
    surplus, given = total - reach - (count - 1), [1] * (count - 1)
    while surplus > 0:
        free = [i for i in range(count - 1) if given[i] < reach]
        whole, remaining = sum([loads[i] for i in free]), surplus
        for i in free:
            addition = min(reach - given[i], max(1, remaining * loads[i] // whole), surplus)
            given[i] = given[i] + addition
            surplus = surplus - addition
    return np.array([reach] + given)


def uneven_parts(rng, amount, total, bound, lean):
    if amount == 2:
        one = jax.random.randint(rng, (), max(1, total - bound), min(bound, total - 1) + 1)
        return jnp.stack([one, total - one])
    lengths = jnp.asarray(length_profile(amount, total, bound, lean), jnp.int32)
    couples = (amount - 1) // 2
    giver, receiver = lengths[1:1 + 2 * couples:2], lengths[2:2 + 2 * couples:2]
    slack = jnp.minimum(giver - 1, bound - receiver)
    shifted = jax.random.randint(jax.random.fold_in(rng, 1), (couples,), 0, 1 << 20) % (slack + 1)
    lengths = lengths.at[1:1 + 2 * couples:2].set(giver - shifted).at[2:2 + 2 * couples:2].set(receiver + shifted)
    return lengths[jax.random.permutation(jax.random.fold_in(rng, 2), amount)]


def assign_block(rng, own, number, rows, count, top, most, lean):
    ranking = jax.random.permutation(rng, count)
    heavy_load, common = load_shares(count, rows * top, most, lean, True), load_shares(count, rows * top, most, lean, False)
    places = jnp.arange(count)

    def named(lengths, rotation):
        used = int((lengths > 0).sum())
        fixed = max(1, used // 4)
        moved = fixed + (places - fixed + rotation * (used - fixed)) % max(1, count - fixed)
        return jnp.zeros((count,), jnp.int32).at[ranking[jnp.where(places < fixed, places, moved)]].set(jnp.asarray(lengths, jnp.int32))

    lengths = jnp.where(number % 4 == 0, named(heavy_load, number // 4), named(common, number - number // 4 - 1))
    mixed = jax.random.permutation(jax.random.fold_in(own, 3), count)
    giver, receiver = mixed[0:count // 2 * 2:2], mixed[1:count // 2 * 2:2]
    slack = jnp.minimum(lengths[giver] - 1, most - lengths[receiver]) // 2
    slack = jnp.where((giver == ranking[0]) | (receiver == ranking[0]) | (lengths[receiver] == 0), 0, jnp.maximum(slack, 0))
    moved = jax.random.randint(jax.random.fold_in(own, 4), (count // 2,), 0, 1 << 20) % (slack + 1)
    lengths = lengths.at[giver].add(-moved).at[receiver].add(moved)
    labels = jnp.searchsorted(jnp.cumsum(lengths), jnp.arange(rows * top), side="right").astype(jnp.int32)
    listing = labels.reshape(top, rows).T
    listing = listing[jax.random.permutation(jax.random.fold_in(own, 1), rows)]
    rotation = jax.random.randint(jax.random.fold_in(own, 2), (rows, 1), 0, top)
    return jnp.take_along_axis(listing, (jnp.arange(top)[None, :] + rotation) % top, axis=1)


def load_shares(count, total, most, lean, full):
    weights = [(1 << 20) // math.isqrt(rank ** lean) + 1 for rank in range(1, count + 1)]
    largest = most if full else min(most, max(-(-total // count), total * weights[0] // sum(weights)))
    least = 1 if total - largest >= count - 1 else 0
    given, spare = [largest] + [least] * (count - 1), total - largest - least * (count - 1)
    while spare > 0:
        movable = [i for i in range(1, count) if given[i] < largest] or [i for i in range(1, count) if given[i] < most]
        pool, left = sum([weights[i] for i in movable]), spare
        for i in movable:
            more = min(most - given[i], max(1, left * weights[i] // pool), spare)
            given[i] = given[i] + more
            spare = spare - more
    return np.array(given)


def noise(rng, extent, width, bound, pieces=(), kind=jnp.bfloat16):
    entries = width * jax.random.normal(rng, extent, jnp.float32)
    if pieces:
        entries = entries * levels(rng, extent, pieces, -0.22, 0.18)
    return jnp.clip(entries, -bound, bound).astype(kind)


def setup_inputs(seed: int = 0) -> dict:
    seeds = jax.random.split(jax.random.key(seed), 7)
    x_slots = noise(seeds[0], (N_DP * SLOT_CAPACITY, D), 1.0, 6.0, ((0, 64), (1, 8)))
    counts = uneven_parts(seeds[1], N_DP, LOST_TOKENS, SLOT_CAPACITY, 2).astype(jnp.int32)
    w_fc1 = noise(seeds[2], (FF, D), D ** -0.5, 0.0546875, ((0, 64), (1, 8)))
    b_fc1 = noise(seeds[3], (FF,), 0.5, 3.0, ((0, 64),), jnp.float32)
    upstream = noise(seeds[4], (N_DP * SLOT_CAPACITY, FF), 1.0, 6.0, ((0, 64),))
    owners_keys = jax.random.split(jax.random.fold_in(seeds[5], 1), (N_DP * GB) // GB)
    owners_turns = jax.random.permutation(jax.random.fold_in(seeds[5], 3), (N_DP * GB) // GB)
    owners = jax.vmap(lambda own, number: assign_block(jax.random.fold_in(seeds[5], 2), own, number, GB, N_DP, 1, MOST, 1))(owners_keys, owners_turns).reshape((N_DP * GB, 1))
    return {"x_slots": x_slots, "counts": counts, "w_fc1": w_fc1, "b_fc1": b_fc1, "upstream": upstream, "owners": owners}


def gelu_slope(values):
    inner_arg = 0.7978845608 * (values + 0.044715 * values * values * values)
    tangent = jnp.tanh(inner_arg)
    return 0.5 * (1.0 + tangent) + 0.5 * values * (1.0 - tangent * tangent) * 0.7978845608 * (1.0 + 3.0 * 0.044715 * values * values)


def reference(x_slots, counts, w_fc1, b_fc1, upstream, owners):
    totals = jnp.cumsum(counts).astype(jnp.int32)
    start_positions = (totals - counts).astype(jnp.int32)
    tokens = jnp.arange(LOST_TOKENS, dtype=jnp.int32)
    holder = jnp.sum((totals[None, :] <= tokens[:, None]).astype(jnp.int32), axis=1).astype(jnp.int32)
    within = (tokens - start_positions[holder]).astype(jnp.int32)
    slot_index = (holder * SLOT_CAPACITY + within).astype(jnp.int32)
    token_rows = x_slots[slot_index]
    token_grads = upstream[slot_index]
    pre = jnp.dot(token_rows, w_fc1.T, preferred_element_type=jnp.float32) + b_fc1
    grad_pre = token_grads.astype(jnp.float32) * gelu_slope(pre)
    grad_low = grad_pre.astype(jnp.bfloat16)
    grad_bias = jnp.sum(grad_pre, axis=0)
    grad_weight = jnp.dot(grad_low.T, token_rows, preferred_element_type=jnp.float32).astype(jnp.bfloat16)
    grad_tokens = jnp.dot(grad_low, w_fc1, preferred_element_type=jnp.float32).astype(jnp.bfloat16)
    slot_numbers = jnp.arange(N_DP * SLOT_CAPACITY, dtype=jnp.int32)
    remaining_replica = slot_numbers // SLOT_CAPACITY
    slot_position = slot_numbers % SLOT_CAPACITY
    active_token_rows = slot_position < counts[remaining_replica]
    token_for_slot = jnp.clip(start_positions[remaining_replica] + slot_position, 0, LOST_TOKENS - 1).astype(jnp.int32)
    grad_slots = jnp.where(active_token_rows[:, None], grad_tokens[token_for_slot], jnp.zeros((), jnp.bfloat16))
    owner_flat = owners[:, 0].astype(jnp.int32)
    same_owner = owner_flat.reshape(N_DP, GB)
    block_order = jnp.arange(GB, dtype=jnp.int32)
    earlier = (same_owner[:, :, None] == same_owner[:, None, :]) & (block_order[None, None, :] < block_order[None, :, None])
    block_rank = jnp.sum(earlier.astype(jnp.int32), axis=2).reshape(-1).astype(jnp.int32)
    old_owner = (jnp.arange(N_DP * GB, dtype=jnp.int32) // GB).astype(jnp.int32)
    blocks = grad_weight.reshape(N_DP * GB, BR, D)
    moved_blocks = jnp.zeros((N_DP, N_DP, MOST, BR, D), jnp.bfloat16).at[owner_flat, old_owner, block_rank].set(blocks)
    return grad_slots, grad_bias, moved_blocks.reshape(N_DP * N_DP * MOST, BR, D)
```

```python
import functools

import jax
import jax.numpy as jnp
from jax import lax
from jax.experimental import pallas as pl
from jax.experimental.pallas import tpu as pltpu
from jax.sharding import Mesh, PartitionSpec as P

BF, F32, I32 = jnp.bfloat16, jnp.float32, jnp.int32
MOST = 2
BR = 6
SLOTS = 10
LOST = 320
HALF = 512
INTERPRET = False


def iota(shape, dim):
    return lax.broadcasted_iota(I32, shape, dim)


def onehot(mask):
    return jnp.where(mask, 1.0, 0.0).astype(BF)


def dot(a, b):
    return jnp.dot(a, b, preferred_element_type=F32)


def dot_nt(a, b):
    return lax.dot_general(a, b, (((1,), (1,)), ((), ())), preferred_element_type=F32)


def call(kernel, outs, args, scalars=0, scratch=()):
    specs = [pl.BlockSpec(memory_space=pltpu.SMEM)] * scalars
    specs += [pl.BlockSpec(memory_space=pltpu.VMEM)] * (len(args) - scalars)
    return pl.pallas_call(
        kernel,
        out_shape=[jax.ShapeDtypeStruct(s, d) for s, d in outs],
        in_specs=specs,
        out_specs=[pl.BlockSpec(memory_space=pltpu.VMEM)] * len(outs),
        scratch_shapes=list(scratch),
        compiler_params=pltpu.CompilerParams(vmem_limit_bytes=44 * 1024 * 1024),
        interpret=INTERPRET,
    )(*args)


def pack_kernel(nz, share, place, x_ref, up_ref, out_ref, rows, ups):
    hid = ups.shape[1] // 2
    tensor = place[0]
    rows[...] = jnp.zeros_like(rows)
    rows[0:SLOTS, :] = x_ref[...]
    ups[...] = jnp.zeros_like(ups)
    for n in range(2 * nz):
        ups[n * 16 : n * 16 + SLOTS, :] = up_ref[:, n * 2 * hid : (n + 1) * 2 * hid]
    k, lane = iota((2 * hid, 128), 0), iota((2 * hid, 128), 1)
    second = lane >= 64
    pick = (k - jnp.where(second, hid, 0)) == tensor * share + lane - jnp.where(second, 64, 0)
    pick = pick & (lane - jnp.where(second, 64, 0) < share)
    chosen = dot(ups[...], onehot(pick)).astype(BF)
    r, c = iota((16, 16), 0), iota((16, 16), 1)
    same = onehot((r == c) & (r < SLOTS))
    even = onehot(c == 2 * (r - SLOTS))
    odd = onehot(c == 2 * (r - SLOTS) + 1)
    a, b, last = rows[:, :HALF], rows[:, HALF : 2 * HALF], rows[:, 2 * HALF :]
    left = (dot(same, a) + dot(even, last)).astype(BF)
    right = (dot(same, b) + dot(odd, last)).astype(BF)
    for z in range(nz):
        out_ref[z, :, :HALF] = left
        out_ref[z, :, HALF : 2 * HALF] = right
        for p in range(2):
            n = 2 * z + p
            out_ref[z, :, 2 * HALF + p * 128 : 2 * HALF + (p + 1) * 128] = chosen[n * 16 : n * 16 + 16]


def spread_kernel(nx, in_ref, out_ref):
    for x in range(nx):
        p = x // 2
        out_ref[x, :, : 2 * HALF] = in_ref[:, : 2 * HALF]
        out_ref[x, :, 2 * HALF :] = in_ref[:, 2 * HALF + p * 128 : 2 * HALF + (p + 1) * 128]


def slot_of(rho, nz, nx):
    xs = rho // (nz * 16)
    zs = (rho // 16) % nz
    return zs * nx + xs, rho % 16


def mask_kernel(nz, nx, row_ref, col_ref, c_ref, ct_ref):
    n = nz * nx
    tokens, total = c_ref.shape[1], c_ref.shape[2]
    for flat in (True, False):
        if flat:
            shape, dim = (n, total), 1
            counts = row_ref[...].astype(BF)
        else:
            shape, dim = (total, n), 0
            counts = col_ref[...].astype(BF)
        s, _ = slot_of(iota(shape, dim), nz, nx)
        other = iota(shape, 1 - dim)
        before, here = onehot(other < s), onehot(other == s)
        if flat:
            start, count = dot(counts, before)[0:1], dot(counts, here)[0:1]
            vec, grid, tdim = (1, total), (tokens, total), 0
        else:
            start, count = dot(before, counts)[:, 0:1], dot(here, counts)[:, 0:1]
            vec, grid, tdim = (total, 1), (total, tokens), 1
        row = iota(vec, dim) % 16
        start, count = start.astype(I32), count.astype(I32)
        token = iota(grid, tdim)
        for i in range(3):
            r = row if i == 0 else 2 * (row - SLOTS) + (i - 1)
            fits = (r >= 0) & (r < count)
            fits = fits & (row < SLOTS) if i == 0 else fits & (row >= SLOTS)
            where = jnp.where(fits, start + r, -1)
            (c_ref if flat else ct_ref)[i] = onehot(where == token)


def pre_kernel(share, place, rb_ref, c_ref, w_ref, xc_ref, ug_ref, part_ref):
    left, right = rb_ref[:, :HALF], rb_ref[:, HALF : 2 * HALF]
    xc_ref[:, :HALF] = dot(c_ref[0], left).astype(BF)
    xc_ref[:, HALF : 2 * HALF] = dot(c_ref[0], right).astype(BF)
    xc_ref[:, 2 * HALF :] = (dot(c_ref[1], left) + dot(c_ref[2], right)).astype(BF)
    part_ref[...] = dot_nt(w_ref[...], xc_ref[...]).astype(BF)
    ups = dot(c_ref[0], rb_ref[:, 2 * HALF :]).T
    ug_ref[...] = jnp.where(place[0] == 1, ups[64 : 64 + share], ups[:share])


def gelu_slope(values):
    inner_arg = 0.7978845608 * (values + 0.044715 * values * values * values)
    tangent = jnp.tanh(inner_arg)
    return 0.5 * (1.0 + tangent) + 0.5 * values * (1.0 - tangent * tangent) * 0.7978845608 * (
        1.0 + 3.0 * 0.044715 * values * values
    )


def grad_kernel(place, parts_ref, ug_ref, b_ref, out_ref):
    share, tokens = out_ref.shape
    hid = b_ref.shape[1]
    wanted = iota((share, hid), 1) == place[0] * share + iota((share, hid), 0)
    bias = jnp.sum(jnp.where(wanted, b_ref[...], 0.0), axis=1, keepdims=True)
    pre = bias + parts_ref[0].astype(F32)
    for j in range(1, parts_ref.shape[0]):
        pre = pre + parts_ref[j].astype(F32)
    lane = iota((share, tokens), 1)
    grad = jnp.where(lane < LOST, ug_ref[...] * gelu_slope(pre), 0.0)
    total = jnp.sum(grad, axis=1, keepdims=True)
    high = total.astype(BF).astype(F32)
    mid = (total - high).astype(BF).astype(F32)
    low = total - high - mid
    grad = jnp.where(lane == LOST, high, grad)
    grad = jnp.where(lane == LOST + 1, mid, grad)
    grad = jnp.where(lane == LOST + 2, low, grad)
    out_ref[...] = grad.astype(BF)


def token_share(tokens, span, place, a, flip):
    shape, td = ((tokens, 128), 0) if not flip else ((128, tokens), 1)
    token, lane = iota(shape, td), iota(shape, 1 - td)
    inside = (lane >= a * span) & (lane < (a + 1) * span)
    return onehot(inside & (token == place * span + lane - a * span))


def out_kernel(nz, nx, span, place, g_ref, ct_ref, w_ref, oc_ref, or_ref, px_ref, bias_ref):
    hid, tokens = g_ref.shape
    total = px_ref.shape[0]
    blocks = oc_ref.shape[0]
    g = g_ref[...]
    pieces = iota((8, tokens), 1)
    bias_ref[...] = dot_nt(onehot((pieces >= LOST) & (pieces < LOST + 3)), g)
    here = [dot_nt(ct_ref[i], g).astype(BF) for i in range(3)]
    last = w_ref[:, 2 * HALF :]
    px_ref[:, :HALF] = (dot(here[0], w_ref[:, :HALF]) + dot(here[1], last)).astype(BF)
    px_ref[:, HALF : 2 * HALF] = (dot(here[0], w_ref[:, HALF : 2 * HALF]) + dot(here[2], last)).astype(BF)
    r, c = iota((blocks, blocks), 0), iota((blocks, blocks), 1)
    owner = or_ref[0:1, :]
    earlier = (oc_ref[:, 0:1] == owner) & (r < c)
    rank = jnp.sum(jnp.where(earlier, 1.0, 0.0), axis=0, keepdims=True)
    target = jnp.broadcast_to(owner * MOST + rank, (8, blocks)).astype(BF)
    block, unit = iota((blocks, hid), 0), iota((blocks, hid), 1)
    within = unit - block * BR
    member = (within >= 0) & (within < BR)
    offset = jnp.sum(jnp.where(member, within, 0).astype(F32), axis=0, keepdims=True)
    key = dot(target, onehot(member))[0:1] * BR + offset
    rho = iota((total, 1), 0)
    dest, row = slot_of(rho, nz, nx)
    q = row % 4
    tile = jnp.zeros((total, 128), F32)
    for a in range(BR // 2):
        wanted = (dest * MOST + q % 2) * BR + 2 * a + q // 2
        wanted = jnp.where(row // 4 == place[1], wanted, -1).astype(F32)
        part = dot(g, token_share(tokens, span, place[0], a, False)).astype(BF)
        tile = tile + dot(onehot(wanted == key), part)
    px_ref[:, 2 * HALF :] = tile.astype(BF)


def sum_kernel(in_ref, out_ref):
    total = in_ref[0].astype(F32)
    for x in range(1, in_ref.shape[0]):
        total = total + in_ref[x].astype(F32)
    out_ref[...] = total.astype(BF)


def slots_kernel(in_ref, out_ref, moved_ref):
    nz = in_ref.shape[0]
    total = in_ref[0, :, : 2 * HALF].astype(F32)
    for z in range(1, nz):
        total = total + in_ref[z, :, : 2 * HALF].astype(F32)
    total = total.astype(BF)
    left, right = total[:, :HALF], total[:, HALF:]
    r, c = iota((16, 16), 0), iota((16, 16), 1)
    halfway = (c - SLOTS) * 2
    last = dot(onehot(r == halfway), left) + dot(onehot(r == halfway + 1), right)
    out_ref[:, : 2 * HALF] = total[:SLOTS]
    out_ref[:, 2 * HALF :] = last[:SLOTS].astype(BF)
    for z in range(nz):
        moved_ref[z * 16 : (z + 1) * 16, :] = in_ref[z, :, 2 * HALF :]


def weight_kernel(span, m_ref, xc_ref, out_ref):
    ranks, total, _ = m_ref.shape
    tokens = xc_ref.shape[0]
    half = total // 2
    r, c = iota((total, total), 0), iota((total, total), 1)
    low, place = r // half, r % half
    order = onehot(c == (place // 2) * 4 + low * 2 + place % 2)
    xc = xc_ref[...]
    for a in range(BR // 2):
        rows = jnp.zeros((total, tokens), F32)
        for j in range(ranks):
            rows = rows + dot(m_ref[j], token_share(tokens, span, j, a, True))
        rows = dot(order, rows.astype(BF)).astype(BF)
        found = dot(rows, xc).astype(BF)
        out_ref[2 * a] = found[:half]
        out_ref[2 * a + 1] = found[half:]


def body(x_slots, counts, w, bias, upstream, owners):
    nz, nx = lax.axis_size("z"), lax.axis_size("x")
    nt = lax.axis_size(("y", "core"))
    hid = w.shape[0]
    share, span = hid // nt, LOST // nt
    total = nx * nz * 16
    tokens = -(-(LOST + 3) // 128) * 128
    dp = nz * nx
    tensor = lax.axis_index(("y", "core")).astype(I32)
    x_me = lax.axis_index("x").astype(I32)

    packed, = call(
        functools.partial(pack_kernel, nz, share),
        [((nz, 16, 2 * HALF + 256), BF)],
        [tensor[None], x_slots, upstream],
        1,
        [pltpu.VMEM((16, 3 * HALF), BF), pltpu.VMEM((2 * nz * 16, 2 * hid), BF)],
    )
    counts = counts.astype(F32)
    c, ct = call(
        functools.partial(mask_kernel, nz, nx),
        [((3, tokens, total), BF), ((3, total, tokens), BF)],
        [jnp.broadcast_to(counts[None, :], (8, dp)), jnp.broadcast_to(counts[:, None], (dp, 128))],
    )
    along_z = lax.all_to_all(packed, "z", 0, 0, tiled=True)
    spread, = call(
        functools.partial(spread_kernel, nx),
        [((nx, nz * 16, 2 * HALF + 128), BF)],
        [along_z.reshape(nz * 16, 2 * HALF + 256)],
    )
    along_x = lax.all_to_all(spread, "x", 0, 0, tiled=True)
    xc, ug, part = call(
        functools.partial(pre_kernel, share),
        [((tokens, 3 * HALF), BF), ((share, tokens), F32), ((hid, tokens), BF)],
        [(x_me % 2)[None], along_x.reshape(total, 2 * HALF + 128), c, w],
        1,
    )
    parts = lax.all_to_all(part.reshape(nt, share, tokens), ("y", "core"), 0, 0, tiled=True)
    low, = call(
        grad_kernel,
        [((share, tokens), BF)],
        [tensor[None], parts, ug, bias[None, :]],
        1,
    )
    grad = lax.all_gather(low, ("y", "core"), axis=0, tiled=True)
    owner = owners[:, 0].astype(F32)
    blocks = owner.shape[0]
    px, grad_bias = call(
        functools.partial(out_kernel, nz, nx, span),
        [((total, 2 * HALF + 128), BF), ((8, hid), F32)],
        [
            jnp.stack([tensor, x_me]),
            grad,
            ct,
            w,
            jnp.broadcast_to(owner[:, None], (blocks, 128)),
            jnp.broadcast_to(owner[None, :], (8, blocks)),
        ],
        1,
    )
    px = lax.all_to_all(px.reshape(nx, nz * 16, 2 * HALF + 128), "x", 0, 0, tiled=True)
    summed, = call(sum_kernel, [((nz * 16, 2 * HALF + 128), BF)], [px])
    pz = lax.all_to_all(summed.reshape(nz, 16, 2 * HALF + 128), "z", 0, 0, tiled=True)
    grad_slots, moved = call(
        slots_kernel, [((SLOTS, 3 * HALF), BF), ((nz * 16, 128), BF)], [pz]
    )
    moved = lax.all_gather(moved, ("y", "core"), axis=0)
    found, = call(
        functools.partial(weight_kernel, span),
        [((BR, MOST * dp, 3 * HALF), BF)],
        [moved, xc],
    )
    return grad_slots, grad_bias[0], found.transpose(1, 0, 2)


def solution(mesh):
    devices = mesh.devices
    dp, tensor = devices.shape
    if dp == 64:
        shape = (16, 4, 4, 2)
    else:
        shape = (dp // 4, 4, tensor // 2, 2)
    fine = Mesh(devices.reshape(shape), ("z", "x", "y", "core"))
    rows, cols = ("z", "x"), ("y", "core")
    in_specs = (P(rows, cols), P(), P(rows, cols), P(rows), P(rows, None), P(rows, None))
    out_specs = (P(rows, cols), P(rows), P(rows, None, cols))
    return jax.shard_map(body, mesh=fine, in_specs=in_specs, out_specs=out_specs, check_vma=False)
```

```python
import functools

import jax
import jax.numpy as jnp
from jax import lax
from jax.experimental import pallas as pl
from jax.experimental.pallas import tpu as pltpu
from jax.sharding import Mesh, PartitionSpec as P

BF, F32, I32 = jnp.bfloat16, jnp.float32, jnp.int32
MOST = 2
BR = 6
SLOTS = 10
HALF = 512
NZ, NX, NT = 16, 4, 8
DP = NZ * NX
HID = 384
GROUP = NX * HID
SHARE = GROUP // NT
QUARTER = SHARE // 4
MAIN, TAIL = NZ * 8, NZ * 2
RHO = NZ * 16
PACK = SHARE + QUARTER
LIMIT = 48 * 1024 * 1024


def iota(shape, dim):
    return lax.broadcasted_iota(I32, shape, dim)


def onehot(mask):
    return jnp.where(mask, 1.0, 0.0).astype(BF)


def dot(a, b):
    return jnp.dot(a, b, preferred_element_type=F32)


def dot_nt(a, b):
    return lax.dot_general(a, b, (((1,), (1,)), ((), ())), preferred_element_type=F32)


def call(kernel, outs, args, scalars=0, scratch=(), flops=0, moved=0):
    specs = [pl.BlockSpec(memory_space=pltpu.SMEM)] * scalars
    specs += [pl.BlockSpec(memory_space=pltpu.VMEM)] * (len(args) - scalars)
    return pl.pallas_call(
        kernel,
        out_shape=[jax.ShapeDtypeStruct(s, d) for s, d in outs],
        in_specs=specs,
        out_specs=[pl.BlockSpec(memory_space=pltpu.VMEM)] * len(outs),
        scratch_shapes=list(scratch),
        compiler_params=pltpu.CompilerParams(vmem_limit_bytes=LIMIT),
        cost_estimate=pl.CostEstimate(flops=flops, bytes_accessed=moved, transcendentals=0),
    )(*args)


def pack_kernel(place, x_ref, up_ref, out_ref, rows, ups):
    rows[...] = jnp.zeros_like(rows)
    rows[0:SLOTS, :] = x_ref[...]
    ups[...] = jnp.zeros_like(ups)
    for z in range(NZ):
        ups[z * 16 : z * 16 + SLOTS, :] = up_ref[:, z * GROUP : (z + 1) * GROUP]
    k, lane = iota((GROUP, 256), 0), iota((GROUP, 256), 1)
    chosen = dot(ups[...], onehot((k == place[0] * SHARE + lane) & (lane < SHARE))).astype(BF)
    r, c = iota((16, 16), 0), iota((16, 16), 1)
    same = onehot((r == c) & (r < SLOTS))
    even = onehot(c == 2 * (r - SLOTS))
    odd = onehot(c == 2 * (r - SLOTS) + 1)
    a, b, last = rows[:, :HALF], rows[:, HALF : 2 * HALF], rows[:, 2 * HALF :]
    left = (dot(same, a) + dot(even, last)).astype(BF)
    right = (dot(same, b) + dot(odd, last)).astype(BF)
    for z in range(NZ):
        out_ref[z, :, :HALF] = left
        out_ref[z, :, HALF : 2 * HALF] = right
        out_ref[z, :, 2 * HALF :] = chosen[z * 16 : z * 16 + 16]


def slot_of(i):
    tail = (i - MAIN) % TAIL
    return jnp.where(i < MAIN, i // 8, tail // 2), jnp.where(i < MAIN, i % 8, 8 + tail % 2)


def selector(third, flip=False):
    i, rho = iota((256, RHO), 1 if flip else 0), iota((256, RHO), 0 if flip else 1)
    z, slot = slot_of(i)
    if third == 0:
        return onehot(rho == z * 16 + slot)
    return onehot((rho == z * 16 + SLOTS + slot // 2) & (slot % 2 == third - 1))


def by_quarter(pieces):
    lane = iota((QUARTER, 128), 1) // 32
    found = jnp.where(lane == 0, pieces[0], 0.0)
    for g in range(1, 4):
        found = jnp.where(lane == g, pieces[g], found)
    return found


def rows_kernel(rz_ref, x_ref, ug_ref):
    left, right = rz_ref[:, :HALF], rz_ref[:, HALF : 2 * HALF]
    first = selector(0)
    x_ref[:, :HALF] = dot(first, left).astype(BF)
    x_ref[:, HALF : 2 * HALF] = dot(first, right).astype(BF)
    x_ref[:, 2 * HALF :] = (dot(selector(1), left) + dot(selector(2), right)).astype(BF)
    ups = dot(first, rz_ref[:, 2 * HALF :])
    main, tail = ups[:MAIN].T, ups[MAIN:].T
    ug_ref[:SHARE, :] = main[:SHARE]
    ug_ref[SHARE:, :] = by_quarter([tail[g * QUARTER : (g + 1) * QUARTER] for g in range(4)])


def pre_kernel(w_ref, x_ref, out_ref):
    x = x_ref[...]
    for j in range(NT):
        found = dot_nt(w_ref[j * SHARE : (j + 1) * SHARE, :], x)
        out_ref[j, :SHARE, :] = found[:, :MAIN].astype(BF)
        tail = [found[g * QUARTER : (g + 1) * QUARTER, MAIN:] for g in range(4)]
        out_ref[j, SHARE:, :] = by_quarter(tail).astype(BF)


def gelu_slope(values):
    inner_arg = 0.7978845608 * (values + 0.044715 * values * values * values)
    tangent = jnp.tanh(inner_arg)
    return 0.5 * (1.0 + tangent) + 0.5 * values * (1.0 - tangent * tangent) * 0.7978845608 * (
        1.0 + 3.0 * 0.044715 * values * values
    )


def grad_kernel(place, parts_ref, ug_ref, side_ref, counts_ref, out_ref):
    tensor, x_me = place[0], place[1]
    side = side_ref[tensor // 2]
    bias = jnp.concatenate([side[1:2], side[2:3], side[3:4]], axis=1)
    wanted = iota((SHARE, HID), 1) == (tensor % 2) * SHARE + iota((SHARE, HID), 0)
    bias = jnp.sum(jnp.where(wanted, bias, 0.0), axis=1, keepdims=True)
    counts = counts_ref[...].astype(BF)
    s = iota((DP, 128), 0)
    lane = iota((DP, 128), 1)
    many = dot(counts, onehot(s == lane // 8 * NX + x_me))[0:1]
    few = dot(counts, onehot(s == lane % TAIL // 2 * NX + x_me))[0:1]
    lane = iota((1, 128), 1)
    many = (lane % 8).astype(F32) < many
    few = (8 + lane % 2).astype(F32) < few
    pre = parts_ref[0].astype(F32)
    for j in range(1, NT):
        pre = pre + parts_ref[j].astype(F32)
    tail_bias = by_quarter([bias[g * QUARTER : (g + 1) * QUARTER] for g in range(4)])
    main = jnp.where(many, ug_ref[:SHARE] * gelu_slope(pre[:SHARE] + bias), 0.0)
    tail = jnp.where(few, ug_ref[SHARE:] * gelu_slope(pre[SHARE:] + tail_bias), 0.0)
    out_ref[:SHARE, :] = main.astype(BF)
    out_ref[SHARE:PACK, :] = tail.astype(BF)
    lane = iota((QUARTER, 128), 1) // 32
    total = jnp.sum(main, axis=1, keepdims=True) + jnp.concatenate(
        [jnp.sum(jnp.where(lane == g, tail, 0.0), axis=1, keepdims=True) for g in range(4)], axis=0
    )
    high = total.astype(BF).astype(F32)
    mid = (total - high).astype(BF).astype(F32)
    low = total - high - mid
    lane = iota((SHARE, 128), 1)
    pieces = jnp.where(lane == 0, high, jnp.where(lane == 1, mid, jnp.where(lane == 2, low, 0.0)))
    pieces = jnp.concatenate([pieces, jnp.zeros((256 - SHARE, 128), F32)], axis=0).T
    out_ref[PACK : PACK + 16, :] = pieces[:16, :128].astype(BF)
    out_ref[PACK + 16 :, :] = pieces[:16, 128:].astype(BF)


def unpacked(tail):
    lane = iota((QUARTER, 128), 1) // 32
    zero = jnp.zeros((), BF)
    return jnp.concatenate([jnp.where(lane == g, tail, zero) for g in range(4)], axis=0)


def moved_kernel(place, g_ref, side_ref, out_ref):
    tensor, x_me = place[0], place[1]
    old, m = tensor // 2, tensor % 2
    blocks = HID // BR
    owner = side_ref[old][0:1, :blocks]
    r, c = iota((blocks, blocks), 0), iota((blocks, blocks), 1)
    column = jnp.sum(jnp.where(r == c, owner, 0.0), axis=1, keepdims=True)
    rank = jnp.sum(jnp.where((column == owner) & (r < c), 1.0, 0.0), axis=0, keepdims=True)
    target = jnp.broadcast_to(owner * MOST + rank, (8, blocks)).astype(BF)
    block, unit = iota((blocks, HID), 0), iota((blocks, HID), 1)
    within = unit - block * BR
    member = (within >= 0) & (within < BR)
    offset = jnp.sum(jnp.where(member, within, 0).astype(F32), axis=0, keepdims=True)
    key = dot(target, onehot(member))[0:1] * BR + offset
    both = [g_ref[2 * old], g_ref[2 * old + 1]]
    main = jnp.concatenate([g[:SHARE] for g in both], axis=0)
    tail = jnp.concatenate([unpacked(g[SHARE:PACK]) for g in both], axis=0)
    r, c = iota((128, 128), 0), iota((128, 128), 1)
    tail = dot(tail, onehot((r % TAIL == c % TAIL) & (c // TAIL == x_me))).astype(BF)
    i = iota((BR * NZ, 1), 0)
    for x in range(NX):
        wanted = (((i % NZ) * NX + x) * MOST + m) * BR + i // NZ
        pick = onehot(wanted.astype(F32) == key)
        out_ref[x, : BR * NZ, :] = dot(pick, main).astype(BF)
        out_ref[x, BR * NZ : 2 * BR * NZ, :] = dot(pick, tail).astype(BF)
        out_ref[x, 2 * BR * NZ : 2 * BR * NZ + 32, :] = g_ref[2 * x, PACK:, :]
        out_ref[x, 2 * BR * NZ + 32 :, :] = g_ref[2 * x + 1, PACK:, :]


def out_kernel(g_ref, w_ref, px_ref, full):
    for j in range(NT):
        full[j * SHARE : (j + 1) * SHARE, :MAIN] = g_ref[j, :SHARE, :]
        full[j * SHARE : (j + 1) * SHARE, MAIN:] = unpacked(g_ref[j, SHARE:PACK, :])
    g = full[...]
    here = [dot_nt(selector(i, True), g).astype(BF) for i in range(3)]
    last = w_ref[:, 2 * HALF :]
    px_ref[:, :HALF] = (dot(here[0], w_ref[:, :HALF]) + dot(here[1], last)).astype(BF)
    px_ref[:, HALF:] = (dot(here[0], w_ref[:, HALF : 2 * HALF]) + dot(here[2], last)).astype(BF)


def join_kernel(px_ref, rx_ref, out_ref, bias_ref):
    out_ref[:, : 2 * HALF] = px_ref[...]
    n = BR * NZ
    rho, k = iota((RHO, 2 * n), 0), iota((RHO, 2 * n), 1)
    z, row = rho // 16, rho % 16
    main = k < n
    k = jnp.where(main, k, k - n)
    b = k // NZ
    here = z == k % NZ
    tiles = [jnp.zeros((RHO, 128), F32), jnp.zeros((RHO, 128), F32)]
    for x in range(NX):
        value = rx_ref[x, : 2 * n, :]
        v = jnp.where(main, x * BR + b, 24 + b)
        for t in range(2):
            tiles[t] = tiles[t] + dot(onehot(here & (v == t * 16 + row)), value)
    out_ref[:, 2 * HALF : 2 * HALF + 128] = tiles[0].astype(BF)
    out_ref[:, 2 * HALF + 128 :] = tiles[1].astype(BF)
    for i in range(4):
        total = jnp.zeros((16, 128), F32)
        for x in range(NX):
            total = total + rx_ref[x, 2 * n + 16 * i : 2 * n + 16 * (i + 1), :].astype(F32)
        bias_ref[i : i + 1, :] = total[2:3] + total[1:2] + total[0:1]


def slots_kernel(in_ref, out_ref, moved_ref):
    total = in_ref[0, :, : 2 * HALF].astype(F32)
    for z in range(1, NZ):
        total = total + in_ref[z, :, : 2 * HALF].astype(F32)
    total = total.astype(BF)
    left, right = total[:, :HALF], total[:, HALF:]
    r, c = iota((16, 16), 0), iota((16, 16), 1)
    halfway = (c - SLOTS) * 2
    last = dot(onehot(r == halfway), left) + dot(onehot(r == halfway + 1), right)
    out_ref[:, : 2 * HALF] = total[:SLOTS]
    out_ref[:, 2 * HALF :] = last[:SLOTS].astype(BF)
    for z in range(NZ):
        moved_ref[z * 16 : (z + 1) * 16, :] = in_ref[z, :, 2 * HALF :]


def weight_kernel(m_ref, x_ref, out_ref, found, tails):
    n = BR * NZ
    i, k = iota((n, 2 * RHO), 0), iota((n, 2 * RHO), 1)
    b, here = i // NZ, i % NZ == (k % RHO) // 16
    place = (k // RHO) * 16 + k % 16
    picks = [onehot(here & (place == (x * BR + b if x < NX else 24 + b))) for x in range(NX + 1)]
    for j in range(NT):
        both = jnp.concatenate([m_ref[j, :, :128], m_ref[j, :, 128:]], axis=0)
        for x in range(NX + 1):
            found[j * n : (j + 1) * n, x * 128 : (x + 1) * 128] = dot(picks[x], both).astype(BF)
    r, c = iota((NT * n, NT * n), 0), iota((NT * n, NT * n), 1)
    order = onehot(c == (r % NT) * n + r // NT)
    rows = dot(order, found[...]).astype(BF)
    for x in range(NX):
        tails[x * TAIL : (x + 1) * TAIL, :] = x_ref[x, MAIN:, :]
    for b in range(BR):
        mine = rows[b * MOST * DP : (b + 1) * MOST * DP]
        total = dot(mine[:, NX * 128 :], tails[...])
        for x in range(NX):
            total = total + dot(mine[:, x * 128 : (x + 1) * 128], x_ref[x, :MAIN, :])
        out_ref[b] = total.astype(BF)


def body(x_slots, counts, w, bias, upstream, owners):
    tensor = lax.axis_index(("y", "core")).astype(I32)
    x_me = lax.axis_index("x").astype(I32)
    place = jnp.stack([tensor, x_me])
    groups = lax.all_gather(w, "x", axis=0, tiled=True)
    owner = jnp.pad(owners[:, 0].astype(F32), (0, 128 - DP))
    side = jnp.concatenate([owner[None], bias.reshape(3, 128), jnp.zeros((4, 128), F32)], axis=0)
    side = lax.all_to_all(jnp.broadcast_to(side, (NX, 8, 128)), "x", 0, 0, tiled=True)
    packed, = call(
        pack_kernel,
        [((NZ, 16, 2 * HALF + 256), BF)],
        [place, x_slots, upstream],
        1,
        [pltpu.VMEM((16, 3 * HALF), BF), pltpu.VMEM((RHO, GROUP), BF)],
        2 * RHO * GROUP * 256,
        2 * 10**6,
    )
    along_z = lax.all_to_all(packed, "z", 0, 0, tiled=True)
    rows, ug = call(
        rows_kernel,
        [((256, 3 * HALF), BF), ((PACK, 128), F32)],
        [along_z.reshape(RHO, 2 * HALF + 256)],
        flops=2 * 256 * 256 * 9 * 256,
        moved=2 * 10**6,
    )
    columns = lax.all_gather(rows[: MAIN + TAIL], "x", axis=0)
    part, = call(
        pre_kernel,
        [((NT, PACK, 128), BF)],
        [groups, rows],
        flops=2 * GROUP * 256 * 3 * HALF,
        moved=6 * 10**6,
    )
    parts = lax.all_to_all(part, ("y", "core"), 0, 0, tiled=True)
    low, = call(
        grad_kernel,
        [((PACK + 32, 128), BF)],
        [place, parts, ug, side, jnp.broadcast_to(counts.astype(F32)[None, :], (8, DP))],
        1,
        moved=10**6,
    )
    grad = lax.all_gather(low, ("y", "core"), axis=0)
    sent, = call(
        moved_kernel,
        [((NX, 256, 128), BF)],
        [place, grad, side],
        1,
        flops=2 * 8 * 96 * HID * 128,
        moved=10**6,
    )
    rx = lax.all_to_all(sent, "x", 0, 0, tiled=True)
    px, = call(
        out_kernel,
        [((RHO, 2 * HALF), BF)],
        [grad, groups],
        0,
        [pltpu.VMEM((GROUP, 256), BF)],
        2 * RHO * GROUP * (4 * HALF + 3 * 256),
        6 * 10**6,
    )
    joined, grad_bias = call(
        join_kernel, [((RHO, 2 * HALF + 256), BF), ((4, 128), F32)], [px, rx], moved=2 * 10**6
    )
    pz = lax.all_to_all(joined.reshape(NZ, 16, 2 * HALF + 256), "z", 0, 0, tiled=True)
    grad_slots, moved = call(
        slots_kernel, [((SLOTS, 3 * HALF), BF), ((RHO, 256), BF)], [pz], moved=10**6
    )
    moved = lax.all_gather(moved, ("y", "core"), axis=0)
    found, = call(
        weight_kernel,
        [((BR, MOST * DP, 3 * HALF), BF)],
        [moved, columns],
        0,
        [pltpu.VMEM((NT * BR * NZ, 640), BF), pltpu.VMEM((NX * TAIL, 3 * HALF), BF)],
        2 * 768 * 640 * 1536,
        5 * 10**6,
    )
    rest = SHARE - 128
    grad_bias = jnp.concatenate([grad_bias[0], grad_bias[1, :rest], grad_bias[2], grad_bias[3, :rest]])
    return grad_slots, grad_bias, found.transpose(1, 0, 2)


def solution(mesh):
    fine = Mesh(mesh.devices.reshape(NZ, NX, NT // 2, 2), ("z", "x", "y", "core"))
    rows, cols = ("z", "x"), ("y", "core")
    in_specs = (P(rows, cols), P(), P(rows, cols), P(rows), P(rows, None), P(rows, None))
    out_specs = (P(rows, cols), P(rows), P(rows, None, cols))
    return jax.shard_map(body, mesh=fine, in_specs=in_specs, out_specs=out_specs, check_vma=False)
```

```python
import functools

import jax
import jax.numpy as jnp
from jax import lax
from jax.experimental import pallas as pl
from jax.experimental.pallas import tpu as pltpu
from jax.sharding import Mesh, PartitionSpec as P

BF, F32, I32 = jnp.bfloat16, jnp.float32, jnp.int32
MOST = 2
BR = 6
SLOTS = 10
HALF = 512
NZ, NX, NT = 16, 4, 8
DP = NZ * NX
HID = 384
GROUP = NX * HID
SHARE = GROUP // NT
QUARTER = SHARE // 4
MAIN, TAIL = NZ * 8, NZ * 2
RHO = NZ * 16
PACK = SHARE + QUARTER
SIDE = 16
FIRST = SIDE + SHARE
FULL = SIDE + HID
MOVED = (NX + 1) * BR
LIMIT = 24 * 1024 * 1024


def iota(shape, dim):
    return lax.broadcasted_iota(I32, shape, dim)


def onehot(mask):
    return jnp.where(mask, 1.0, 0.0).astype(BF)


def dot(a, b):
    return jnp.dot(a, b, preferred_element_type=F32)


def dot_nt(a, b):
    return lax.dot_general(a, b, (((1,), (1,)), ((), ())), preferred_element_type=F32)


VMEM, HBM, ANY, SMEM = pltpu.VMEM, pltpu.HBM, pl.ANY, pltpu.SMEM


def call(kernel, outs, args, scalars=0, scratch=(), flops=0, moved=0, outside=(), space=ANY, limit=LIMIT):
    specs = [
        pl.BlockSpec(memory_space=SMEM if i < scalars else space if i in outside else VMEM)
        for i in range(len(args))
    ]
    return pl.pallas_call(
        kernel,
        out_shape=[jax.ShapeDtypeStruct(s, d) for s, d in outs],
        in_specs=specs,
        out_specs=[pl.BlockSpec(memory_space=VMEM)] * len(outs),
        scratch_shapes=list(scratch),
        compiler_params=pltpu.CompilerParams(vmem_limit_bytes=limit),
        cost_estimate=pl.CostEstimate(flops=flops, bytes_accessed=moved, transcendentals=0),
    )(*args)


def pieces_of(value):
    high = value.astype(BF).astype(F32)
    mid = (value - high).astype(BF).astype(F32)
    return high, mid, value - high - mid


def pack_kernel(place, x_in, up_in, w_in, bias_in, owner_in, full_ref, out_ref, x_ref, up_ref, bias_ref, owner_ref, rows, ups, sems):
    copies = [
        pltpu.make_async_copy(source, target, sems.at[i])
        for i, (source, target) in enumerate(
            [
                (up_in, up_ref),
                (x_in, x_ref),
                (bias_in, bias_ref),
                (owner_in, owner_ref),
                (w_in, full_ref.at[pl.ds(SIDE, HID), :]),
            ]
        )
    ]
    for copy in copies:
        copy.start()
    k, lane = iota((GROUP, 256), 0), iota((GROUP, 256), 1)
    pick = onehot((k == place[0] * SHARE + lane) & (lane < SHARE))
    r, c = iota((16, 16), 0), iota((16, 16), 1)
    same = onehot((r == c) & (r < SLOTS))
    even = onehot(c == 2 * (r - SLOTS))
    odd = onehot(c == 2 * (r - SLOTS) + 1)
    rows[...] = jnp.zeros_like(rows)
    ups[...] = jnp.zeros_like(ups)
    copies[0].wait()
    for z in range(NZ):
        ups[z * 16 : z * 16 + SLOTS, :] = up_ref[:, z * GROUP : (z + 1) * GROUP]
    chosen = dot(ups[...], pick).astype(BF)
    copies[1].wait()
    rows[0:SLOTS, :] = x_ref[...]
    a, b, last = rows[:, :HALF], rows[:, HALF : 2 * HALF], rows[:, 2 * HALF :]
    left = (dot(same, a) + dot(even, last)).astype(BF)
    right = (dot(same, b) + dot(odd, last)).astype(BF)
    for z in range(NZ):
        out_ref[z, :, :HALF] = left
        out_ref[z, :, HALF : 2 * HALF] = right
        out_ref[z, :, 2 * HALF :] = chosen[z * 16 : z * 16 + 16]
    copies[2].wait()
    row = iota((SIDE, HID), 0)
    high, mid, low = pieces_of(bias_ref[...].reshape(1, HID))
    side = jnp.where(row == 1, high, jnp.where(row == 2, mid, jnp.where(row == 3, low, 0.0)))
    copies[3].wait()
    owner = jnp.where(iota((SIDE, DP), 0) == 0, owner_ref[...].astype(F32), 0.0).astype(BF)
    owner = dot(owner, onehot(iota((DP, HID), 0) == iota((DP, HID), 1)))
    full_ref[:SIDE, :HID] = (owner + side).astype(BF)
    full_ref[:SIDE, HID:] = jnp.zeros((SIDE, 3 * HALF - HID), BF)
    copies[4].wait()


def sum_rows(total):
    high, mid, low = pieces_of(total)
    lane = iota((SHARE, 128), 1)
    pieces = jnp.where(lane == 0, high, jnp.where(lane == 1, mid, jnp.where(lane == 2, low, 0.0)))
    pieces = jnp.concatenate([pieces, jnp.zeros((256 - SHARE, 128), F32)], axis=0).T[:16].astype(BF)
    r, c = iota((16, 16), 0), iota((16, 16), 1)
    shift = onehot(iota((128, 128), 0) + 64 == iota((128, 128), 1))
    rest = dot(pieces[:, 128:], shift).astype(BF)
    rows = dot(onehot((r == c + 12) & (c < 3)), pieces[:, :128]) + dot(onehot((r == c + 6) & (c < 3)), rest)
    return rows.astype(BF)


def slot_of(i):
    tail = (i - MAIN) % TAIL
    return jnp.where(i < MAIN, i // 8, tail // 2), jnp.where(i < MAIN, i % 8, 8 + tail % 2)


def selector(third, flip=False):
    i, rho = iota((256, RHO), 1 if flip else 0), iota((256, RHO), 0 if flip else 1)
    z, slot = slot_of(i)
    if third == 0:
        return onehot(rho == z * 16 + slot)
    return onehot((rho == z * 16 + SLOTS + slot // 2) & (slot % 2 == third - 1))


def by_quarter(pieces):
    lane = iota((QUARTER, 128), 1) // 32
    found = jnp.where(lane == 0, pieces[0], 0.0)
    for g in range(1, 4):
        found = jnp.where(lane == g, pieces[g], found)
    return found


def rows_kernel(rz_ref, x_ref, column_ref, ug_ref):
    left, right = rz_ref[:, :HALF], rz_ref[:, HALF : 2 * HALF]
    first = selector(0)
    x_ref[:, :HALF] = dot(first, left).astype(BF)
    x_ref[:, HALF : 2 * HALF] = dot(first, right).astype(BF)
    x_ref[:, 2 * HALF :] = (dot(selector(1), left) + dot(selector(2), right)).astype(BF)
    column_ref[...] = x_ref[: MAIN + TAIL, :]
    ups = dot(first, rz_ref[:, 2 * HALF :])
    main, tail = ups[:MAIN].T, ups[MAIN:].T
    ug_ref[:SHARE, :] = main[:SHARE]
    ug_ref[SHARE:, :] = by_quarter([tail[g * QUARTER : (g + 1) * QUARTER] for g in range(4)])


def load(refs, held, sems):
    own, following, first, second, previous = refs
    copies = [
        pltpu.make_async_copy(source, target, sems.at[i])
        for i, (source, target) in enumerate(
            [
                (own, held.at[0]),
                (following, held.at[1]),
                (first, held.at[2, pl.ds(0, FIRST), :]),
                (second, held.at[2, pl.ds(FIRST, SHARE), :]),
                (previous, held.at[3]),
            ]
        )
    ]
    for copy in copies:
        copy.start()
    return [copies[:1], copies[1:2], copies[2:4], copies[4:]]


def pre_kernel(place, x_ref, *refs):
    out_ref, side_ref, held, sems = refs[5:]
    copies = load(refs[:5], held, sems)
    x = x_ref[...]
    for k in range(NX):
        for copy in copies[k]:
            copy.wait()
        source = (place[1] + k) % NX
        side_ref[source] = held[k, :SIDE, :HID].astype(F32)
        for h in range(2):
            start = SIDE + h * SHARE
            j = 2 * source + h
            found = dot_nt(held[k, start : start + SHARE, :], x)
            out_ref[j, :SHARE, :] = found[:, :MAIN].astype(BF)
            tail = [found[g * QUARTER : (g + 1) * QUARTER, MAIN:] for g in range(4)]
            out_ref[j, SHARE:, :] = by_quarter(tail).astype(BF)


def gelu_slope(values):
    inner_arg = 0.7978845608 * (values + 0.044715 * values * values * values)
    tangent = jnp.tanh(inner_arg)
    return 0.5 * (1.0 + tangent) + 0.5 * values * (1.0 - tangent * tangent) * 0.7978845608 * (
        1.0 + 3.0 * 0.044715 * values * values
    )


def grad_kernel(place, parts_ref, ug_ref, side_ref, counts_ref, out_ref, sums_ref):
    tensor, x_me = place[0], place[1]
    side = side_ref[tensor // 2]
    bias = side[1:2] + side[2:3] + side[3:4]
    wanted = iota((SHARE, HID), 1) == (tensor % 2) * SHARE + iota((SHARE, HID), 0)
    bias = jnp.sum(jnp.where(wanted, bias, 0.0), axis=1, keepdims=True)
    counts = jnp.broadcast_to(counts_ref[...].astype(F32), (8, DP)).astype(BF)
    s = iota((DP, 128), 0)
    lane = iota((DP, 128), 1)
    many = dot(counts, onehot(s == lane // 8 * NX + x_me))[0:1]
    few = dot(counts, onehot(s == lane % TAIL // 2 * NX + x_me))[0:1]
    lane = iota((1, 128), 1)
    many = (lane % 8).astype(F32) < many
    few = (8 + lane % 2).astype(F32) < few
    pre = parts_ref[0].astype(F32)
    for j in range(1, NT):
        pre = pre + parts_ref[j].astype(F32)
    tail_bias = by_quarter([bias[g * QUARTER : (g + 1) * QUARTER] for g in range(4)])
    main = jnp.where(many, ug_ref[:SHARE] * gelu_slope(pre[:SHARE] + bias), 0.0)
    tail = jnp.where(few, ug_ref[SHARE:] * gelu_slope(pre[SHARE:] + tail_bias), 0.0)
    out_ref[:SHARE, :] = main.astype(BF)
    out_ref[SHARE:PACK, :] = tail.astype(BF)
    lane = iota((QUARTER, 128), 1) // 32
    total = jnp.sum(main, axis=1, keepdims=True) + jnp.concatenate(
        [jnp.sum(jnp.where(lane == g, tail, 0.0), axis=1, keepdims=True) for g in range(4)], axis=0
    )
    sums_ref[...] = sum_rows(total)


def unpacked(tail):
    lane = iota((QUARTER, 128), 1) // 32
    zero = jnp.zeros((), BF)
    return jnp.concatenate([jnp.where(lane == g, tail, zero) for g in range(4)], axis=0)


def moved_kernel(place, low_ref, other_ref, sums_ref, side_ref, out_ref):
    tensor, x_me = place[0], place[1]
    m = tensor % 2
    blocks = HID // BR
    owner = side_ref[tensor // 2][0:1, :blocks]
    r, c = iota((blocks, blocks), 0), iota((blocks, blocks), 1)
    column = jnp.sum(jnp.where(r == c, owner, 0.0), axis=1, keepdims=True)
    rank = jnp.sum(jnp.where((column == owner) & (r < c), 1.0, 0.0), axis=0, keepdims=True)
    target = jnp.broadcast_to(owner * MOST + rank, (8, blocks)).astype(BF)
    block, unit = iota((blocks, HID), 0), iota((blocks, HID), 1)
    within = unit - block * BR
    member = (within >= 0) & (within < BR)
    offset = jnp.sum(jnp.where(member, within, 0).astype(F32), axis=0, keepdims=True)
    key = dot(target, onehot(member))[0:1] * BR + offset
    low, other = low_ref[...], other_ref[...]
    both = [jnp.where(m == 0, low, other), jnp.where(m == 0, other, low)]
    main = jnp.concatenate([g[:SHARE] for g in both], axis=0)
    tail = jnp.concatenate([unpacked(g[SHARE:PACK]) for g in both], axis=0)
    r, c = iota((128, 128), 0), iota((128, 128), 1)
    tail = dot(tail, onehot((r % TAIL == c) & (c < TAIL))).astype(BF)
    rho = iota((DP * 16, 1), 0)
    dest, row = rho // 16, rho % 16
    wanted = (dest * MOST + m) * BR + row % BR
    wanted = jnp.where(row < 2 * BR, wanted, -1).astype(F32)
    found = dot(onehot(wanted == key), jnp.concatenate([main, tail], axis=1))
    found = jnp.where(row < BR, found[:, :128], found[:, 128:]).astype(BF)
    sums = sums_ref[...]
    for e in range(DP):
        out_ref[e * 16 : (e + 1) * 16, :] = found[e * 16 : (e + 1) * 16] + sums


def out_kernel(place, g_ref, *refs):
    px_ref, full, held, sems = refs[5:]
    copies = load(refs[:5], held, sems)
    for n in range(2 * NX):
        j = (place[1] + n // 2) % NX * 2 + n % 2
        full[n * SHARE : (n + 1) * SHARE, :MAIN] = g_ref[j, :SHARE, :]
        full[n * SHARE : (n + 1) * SHARE, MAIN:] = unpacked(g_ref[j, SHARE:PACK, :])
    g = full[...]
    here = [dot_nt(selector(i, True), g).astype(BF) for i in range(3)]
    total = [jnp.zeros((RHO, HALF), F32), jnp.zeros((RHO, HALF), F32)]
    for k in range(NX):
        for copy in copies[k]:
            copy.wait()
        span = slice(k * HID, (k + 1) * HID)
        last = held[k, SIDE:, 2 * HALF :]
        for side in range(2):
            part = dot(here[0][:, span], held[k, SIDE:, side * HALF : (side + 1) * HALF])
            total[side] = total[side] + part + dot(here[1 + side][:, span], last)
    for side in range(2):
        px_ref[:, side * HALF : (side + 1) * HALF] = total[side].astype(BF)


def order_kernel(place, in_ref, out_ref, block):
    n = BR * NZ
    r, c = iota((2 * n, RHO), 0), iota((2 * n, RHO), 1)
    pick = onehot((c // 16 == r % NZ) & (c % 16 == r // NZ))
    r, c = iota((128, 128), 0), iota((128, 128), 1)
    tail = jnp.zeros((n, 128), F32)
    sums = jnp.zeros((16, 128), F32)
    for x in range(NX):
        for z in range(NZ):
            block[z * 16 : (z + 1) * 16, :] = in_ref[z * NX + x]
        found = dot(pick, block[...]).astype(BF)
        out_ref[x * n : (x + 1) * n, :] = found[:n]
        tail = tail + dot(found[n:], onehot((r < TAIL) & (c == r + x * TAIL)))
        sums = sums + in_ref[place[2] * NX + x].astype(F32)
    out_ref[NX * n : MOVED * NZ, :] = tail.astype(BF)
    row = iota((8, 128), 0)
    for i, first in enumerate((12, 6)):
        total = sums[first + 2 : first + 3] + sums[first + 1 : first + 2] + sums[first : first + 1]
        high, mid, low = pieces_of(total)
        part = jnp.where(row == 0, high, jnp.where(row == 1, mid, jnp.where(row == 2, low, 0.0)))
        parts = part if i == 0 else jnp.concatenate([parts, part], axis=0)
    out_ref[MOVED * NZ :, :] = parts.astype(BF)


def slots_kernel(in_ref, out_ref):
    total = in_ref[0].astype(F32)
    for z in range(1, NZ):
        total = total + in_ref[z].astype(F32)
    total = total.astype(BF)
    left, right = total[:, :HALF], total[:, HALF:]
    r, c = iota((16, 16), 0), iota((16, 16), 1)
    halfway = (c - SLOTS) * 2
    last = dot(onehot(r == halfway), left) + dot(onehot(r == halfway + 1), right)
    out_ref[:, : 2 * HALF] = total[:SLOTS]
    out_ref[:, 2 * HALF :] = last[:SLOTS].astype(BF)


def weight_kernel(place, m_ref, *refs):
    columns, (out_ref, bias_ref, found, tails) = refs[:NX], refs[NX:]
    lane, unit = iota((128, HID), 0), iota((128, HID), 1)
    row = iota((16, 128), 0)
    total = jnp.zeros((16, HID), F32)
    for h in range(2):
        sums = m_ref[place[1] * 2 + h, MOVED * NZ :, :]
        for i in range(2):
            mine = (unit == h * SHARE + i * 64 + lane) & (lane >= i * 64)
            total = total + dot(jnp.where(row // 8 == i, sums, jnp.zeros((), BF)), onehot(mine))
    total = total[:8] + total[8:]
    bias_ref[...] = total[2:3] + total[1:2] + total[0:1]
    n = BR * NZ
    for j in range(NT):
        for k in range(NX + 1):
            start = pl.multiple_of((place[1] + k) % NX * n, n) if k < NX else NX * n
            block = m_ref[j, pl.ds(start, n), :]
            for b in range(BR):
                row = b * MOST * DP + j * NZ
                found[row : row + NZ, k * 128 : (k + 1) * 128] = block[b * NZ : (b + 1) * NZ]
    r, c = iota((MOST * DP, MOST * DP), 0), iota((MOST * DP, MOST * DP), 1)
    order = onehot(c == r % NT * NZ + r // NT)
    for k in range(NX):
        tails[(place[1] + k) % NX] = columns[k][MAIN:, :]
    tail = tails[...].reshape(NX * TAIL, 3 * HALF)
    for b in range(BR):
        mine = dot(order, found[b * MOST * DP : (b + 1) * MOST * DP, :]).astype(BF)
        total = dot(mine[:, NX * 128 :], tail)
        for k in range(NX):
            total = total + dot(mine[:, k * 128 : (k + 1) * 128], columns[k][:MAIN, :])
        out_ref[b] = total.astype(BF)


def hold_kernel(*refs):
    del refs


def hold(arrays):
    return pl.pallas_call(
        hold_kernel,
        out_shape=[jax.ShapeDtypeStruct(a.shape, a.dtype) for a in arrays],
        in_specs=[pl.BlockSpec(memory_space=ANY)] * len(arrays),
        out_specs=[pl.BlockSpec(memory_space=ANY)] * len(arrays),
        input_output_aliases={i: i for i in range(len(arrays))},
        cost_estimate=pl.CostEstimate(flops=50 * 10**9, bytes_accessed=0, transcendentals=0),
    )(*arrays)


def halves_kernel(next_ref, prev_ref, first_ref, second_ref, sems):
    copies = [
        pltpu.make_async_copy(next_ref.at[pl.ds(0, FIRST), :], first_ref, sems.at[0]),
        pltpu.make_async_copy(prev_ref.at[pl.ds(FIRST, SHARE), :], second_ref, sems.at[1]),
    ]
    for copy in copies:
        copy.start()
    for copy in copies:
        copy.wait()


def halves(following, previous):
    return pl.pallas_call(
        halves_kernel,
        out_shape=[jax.ShapeDtypeStruct((n, 3 * HALF), BF) for n in (FIRST, SHARE)],
        in_specs=[pl.BlockSpec(memory_space=ANY)] * 2,
        out_specs=[pl.BlockSpec(memory_space=VMEM)] * 2,
        scratch_shapes=[pltpu.SemaphoreType.DMA((2,))],
        cost_estimate=pl.CostEstimate(flops=50 * 10**9, bytes_accessed=0, transcendentals=0),
    )(following, previous)


def to_left(value):
    return lax.ppermute(value, "x", [(i, (i - 1) % NX) for i in range(NX)])


def to_right(value):
    return lax.ppermute(value, "x", [(i, (i + 1) % NX) for i in range(NX)])


def across(value):
    return lax.ppermute(value, "x", [(i, (i + 2) % NX) for i in range(NX)])


def body(x_slots, counts, w, bias, upstream, owners):
    tensor = lax.axis_index(("y", "core")).astype(I32)
    x_me = lax.axis_index("x").astype(I32)
    place = jnp.stack([tensor, x_me, lax.axis_index("z").astype(I32)])
    full, packed = call(
        pack_kernel,
        [((FULL, 3 * HALF), BF), ((NZ, 16, 2 * HALF + 256), BF)],
        [place, x_slots, upstream, w, bias, owners.reshape(1, DP)],
        1,
        [
            VMEM((SLOTS, 3 * HALF), BF),
            VMEM((SLOTS, NZ * GROUP), BF),
            VMEM((HID,), F32),
            VMEM((1, DP), I32),
            VMEM((16, 3 * HALF), BF),
            VMEM((RHO, GROUP), BF),
            pltpu.SemaphoreType.DMA((5,)),
        ],
        2 * RHO * GROUP * 256,
        5 * 10**6,
        (1, 2, 3, 4, 5),
        HBM,
        56 * 1024 * 1024,
    )
    following, previous = to_left(full), to_right(full)
    along_z = lax.all_to_all(packed, "z", 0, 0, tiled=True)
    first, second = halves(following, previous)
    pieces = [full, following, to_left(first), to_right(second), previous]
    rows, column, ug = call(
        rows_kernel,
        [((256, 3 * HALF), BF), ((MAIN + TAIL, 3 * HALF), BF), ((PACK, 128), F32)],
        [along_z.reshape(RHO, 2 * HALF + 256)],
        flops=2 * 256 * 256 * 9 * 256,
        moved=2 * 10**6,
    )
    part, side = call(
        pre_kernel,
        [((NT, PACK, 128), BF), ((NX, SIDE, HID), F32)],
        [place, rows] + pieces,
        1,
        [VMEM((NX, FULL, 3 * HALF), BF), pltpu.SemaphoreType.DMA((5,))],
        2 * GROUP * 256 * 3 * HALF,
        6 * 10**6,
        range(2, 7),
    )
    columns = [column] + list(hold([to_left(column), across(column), to_right(column)]))
    parts = lax.all_to_all(part, ("y", "core"), 0, 0, tiled=True)
    low, sums = call(
        grad_kernel,
        [((PACK, 128), BF), ((16, 128), BF)],
        [place, parts, ug, side, counts.reshape(1, DP)],
        1,
        moved=10**6,
    )
    other = lax.ppermute(low, "core", [(0, 1), (1, 0)])
    sent, = call(
        moved_kernel,
        [((DP * 16, 128), BF)],
        [place, low, other, sums, side],
        1,
        flops=2 * 8 * 96 * HID * 128,
        moved=10**6,
    )
    moved = lax.all_to_all(sent.reshape(DP, 16, 128), ("z", "x"), 0, 0, tiled=True)
    low, sent = lax.optimization_barrier((low, sent))
    grad = lax.all_gather(low, ("y", "core"), axis=0)
    px, = call(
        out_kernel,
        [((RHO, 2 * HALF), BF)],
        [place, grad] + pieces,
        1,
        [
            VMEM((GROUP, 256), BF),
            VMEM((NX, FULL, 3 * HALF), BF),
            pltpu.SemaphoreType.DMA((5,)),
        ],
        2 * RHO * GROUP * (4 * HALF + 3 * 256),
        6 * 10**6,
        range(2, 7),
    )
    px, moved, *columns = lax.optimization_barrier((px, moved, *columns))
    pz = lax.all_to_all(px.reshape(NZ, 16, 2 * HALF), "z", 0, 0, tiled=True)
    moved, = call(
        order_kernel,
        [((MOVED * NZ + 16, 128), BF)],
        [place, moved],
        1,
        [VMEM((RHO, 128), BF)],
        moved=10**6,
    )
    moved = lax.all_gather(moved, ("y", "core"), axis=0)
    found, grad_bias = call(
        weight_kernel,
        [((BR, MOST * DP, 3 * HALF), BF), ((1, HID), F32)],
        [place, moved] + columns,
        1,
        [VMEM((NT * BR * NZ, 640), BF), VMEM((NX, TAIL, 3 * HALF), BF)],
        2 * 768 * 640 * 1536,
        5 * 10**6,
    )
    grad_slots, = call(slots_kernel, [((SLOTS, 3 * HALF), BF)], [pz], moved=10**6)
    return grad_slots, grad_bias.reshape(HID), found.transpose(1, 0, 2)


def solution(mesh):
    fine = Mesh(mesh.devices.reshape(NZ, NX, NT // 2, 2), ("z", "x", "y", "core"))
    rows, cols = ("z", "x"), ("y", "core")
    in_specs = (P(rows, cols), P(), P(rows, cols), P(rows), P(rows, None), P(rows, None))
    out_specs = (P(rows, cols), P(rows), P(rows, None, cols))
    return jax.shard_map(body, mesh=fine, in_specs=in_specs, out_specs=out_specs, check_vma=False)
```

```python
import functools

import jax
import jax.numpy as jnp
from jax import lax
from jax.experimental import pallas as pl
from jax.experimental.pallas import tpu as pltpu
from jax.sharding import Mesh, PartitionSpec as P

BF, F32, I32 = jnp.bfloat16, jnp.float32, jnp.int32
MOST = 2
BR = 6
SLOTS = 10
HALF = 512
NZ, NX, NT = 16, 4, 8
DP = NZ * NX
HID = 384
GROUP = NX * HID
SHARE = GROUP // NT
QUARTER = SHARE // 4
MAIN, TAIL = NZ * 8, NZ * 2
RHO = NZ * 16
PACK = SHARE + QUARTER
SIDE = 16
FIRST = SIDE + SHARE
FULL = SIDE + HID
MOVED = (NX + 1) * BR
LIMIT = 16 * 1024 * 1024
LARGE = 56 * 1024 * 1024
WIDTH = 2 * HALF + 128


def iota(shape, dim):
    return lax.broadcasted_iota(I32, shape, dim)


def onehot(mask):
    return jnp.where(mask, 1.0, 0.0).astype(BF)


def dot(a, b):
    return jnp.dot(a, b, preferred_element_type=F32)


def dot_nt(a, b):
    return lax.dot_general(a, b, (((1,), (1,)), ((), ())), preferred_element_type=F32)


VMEM, HBM, ANY, SMEM = pltpu.VMEM, pltpu.HBM, pl.ANY, pltpu.SMEM


def call(kernel, outs, args, scalars=0, scratch=(), flops=0, moved=0, outside=(), space=ANY, limit=LIMIT):
    specs = [
        pl.BlockSpec(memory_space=SMEM if i < scalars else space if i in outside else VMEM)
        for i in range(len(args))
    ]
    return pl.pallas_call(
        kernel,
        out_shape=[jax.ShapeDtypeStruct(s, d) for s, d in outs],
        in_specs=specs,
        out_specs=[pl.BlockSpec(memory_space=VMEM)] * len(outs),
        scratch_shapes=list(scratch),
        compiler_params=pltpu.CompilerParams(vmem_limit_bytes=limit),
        cost_estimate=pl.CostEstimate(flops=flops, bytes_accessed=moved, transcendentals=0),
    )(*args)


def pieces_of(value):
    high = value.astype(BF).astype(F32)
    mid = (value - high).astype(BF).astype(F32)
    return high, mid, value - high - mid


def pack_kernel(place, x_in, up_in, w_in, bias_in, owner_in, top_ref, bottom_ref, out_ref, x_ref, up_ref, bias_ref, owner_ref, rows, ups, sems):
    copies = [
        pltpu.make_async_copy(source, target, sems.at[i])
        for i, (source, target) in enumerate(
            [
                (up_in, up_ref),
                (x_in, x_ref),
                (bias_in, bias_ref),
                (owner_in, owner_ref),
                (w_in.at[pl.ds(0, SHARE), :], top_ref.at[pl.ds(SIDE, SHARE), :]),
                (w_in.at[pl.ds(SHARE, SHARE), :], bottom_ref),
            ]
        )
    ]
    for copy in copies:
        copy.start()
    skip = place[0] % 2 * 64
    k, lane = iota((256, 384), 0) - skip, iota((256, 384), 1)
    pick = (lane < 128) & (k == lane)
    pick = pick | ((lane >= 128) & (lane < 192) & (k == lane))
    pick = onehot(pick | ((lane >= 320) & (k == lane - 192)))
    k, lane = iota((RHO, RHO), 0), iota((RHO, RHO), 1)
    block = k // 16 == lane // 16
    k, lane = k % 16, lane % 16
    kept = onehot(block & (k == lane) & (k < SLOTS))
    kept_even = onehot(block & (lane == 2 * (k - SLOTS)))
    kept_odd = onehot(block & (lane == 2 * (k - SLOTS) + 1))
    r, c = iota((16, 16), 0), iota((16, 16), 1)
    same = onehot((r == c) & (r < SLOTS))
    even = onehot(c == 2 * (r - SLOTS))
    odd = onehot(c == 2 * (r - SLOTS) + 1)
    rows[...] = jnp.zeros_like(rows)
    ups[...] = jnp.zeros_like(ups)
    copies[0].wait()
    for z in range(NZ):
        start = pl.multiple_of(z * GROUP + place[0] * 3 // 2 * 128, 128)
        ups[z * 16 : z * 16 + SLOTS, :] = up_ref[:, pl.ds(start, 256)]
    chosen = dot(ups[...], pick).astype(BF)
    chosen = dot(kept, chosen[:, :128]) + dot(kept_even, chosen[:, 128:256]) + dot(kept_odd, chosen[:, 256:])
    chosen = chosen.astype(BF)
    copies[1].wait()
    rows[0:SLOTS, :] = x_ref[...]
    a, b, last = rows[:, :HALF], rows[:, HALF : 2 * HALF], rows[:, 2 * HALF :]
    left = (dot(same, a) + dot(even, last)).astype(BF)
    right = (dot(same, b) + dot(odd, last)).astype(BF)
    for z in range(NZ):
        out_ref[z, :, :HALF] = left
        out_ref[z, :, HALF : 2 * HALF] = right
        out_ref[z, :, 2 * HALF :] = chosen[z * 16 : z * 16 + 16]
    copies[2].wait()
    row = iota((SIDE, HID), 0)
    high, mid, low = pieces_of(bias_ref[...].reshape(1, HID))
    side = jnp.where(row == 1, high, jnp.where(row == 2, mid, jnp.where(row == 3, low, 0.0)))
    copies[3].wait()
    owner = jnp.where(iota((SIDE, DP), 0) == 0, owner_ref[...].astype(F32), 0.0).astype(BF)
    owner = dot(owner, onehot(iota((DP, HID), 0) == iota((DP, HID), 1)))
    top_ref[:SIDE, :HID] = (owner + side).astype(BF)
    top_ref[:SIDE, HID:] = jnp.zeros((SIDE, 3 * HALF - HID), BF)
    copies[4].wait()
    copies[5].wait()


def sum_rows(total):
    high, mid, low = pieces_of(total)
    lane = iota((SHARE, 128), 1)
    pieces = jnp.where(lane == 0, high, jnp.where(lane == 1, mid, jnp.where(lane == 2, low, 0.0)))
    pieces = jnp.concatenate([pieces, jnp.zeros((256 - SHARE, 128), F32)], axis=0).T[:16].astype(BF)
    r, c = iota((16, 16), 0), iota((16, 16), 1)
    shift = onehot(iota((128, 128), 0) + 64 == iota((128, 128), 1))
    rest = dot(pieces[:, 128:], shift).astype(BF)
    head = (c < 3) & (r == jnp.where(c < 2, c + 6, 14))
    rows = dot(onehot(head), pieces[:, :128]) + dot(onehot((r == c + 8) & (c < 3)), rest)
    return rows.astype(BF)


def slot_of(i):
    tail = (i - MAIN) % TAIL
    return jnp.where(i < MAIN, i // 8, tail // 2), jnp.where(i < MAIN, i % 8, 8 + tail % 2)


def selector(third, flip=False):
    i, rho = iota((256, RHO), 1 if flip else 0), iota((256, RHO), 0 if flip else 1)
    z, slot = slot_of(i)
    if third == 0:
        return onehot(rho == z * 16 + slot)
    return onehot((rho == z * 16 + SLOTS + slot // 2) & (slot % 2 == third - 1))


def by_quarter(pieces):
    lane = iota((QUARTER, 128), 1) // 32
    found = jnp.where(lane == 0, pieces[0], 0.0)
    for g in range(1, 4):
        found = jnp.where(lane == g, pieces[g], found)
    return found


def rows_kernel(_, rz_ref, x_ref, column_ref, ug_out, ug_ref):
    left, right, ups = rz_ref[:, :HALF], rz_ref[:, HALF : 2 * HALF], rz_ref[:, 2 * HALF :]
    first, even, odd = selector(0), selector(1), selector(2)
    x_ref[:, :HALF] = dot(first, left).astype(BF)
    x_ref[:, HALF : 2 * HALF] = dot(first, right).astype(BF)
    x_ref[:, 2 * HALF :] = (dot(even, left) + dot(odd, right)).astype(BF)
    r, c = iota((128, 128), 0), iota((128, 128), 1)
    low, high = dot(ups, onehot((r == c) & (r < 64))).astype(BF), dot(ups, onehot(r == c + 64)).astype(BF)
    for part, rest in (
        (dot(first, ups), slice(0, 128)),
        (dot(even, low) + dot(odd, high), slice(128, SHARE)),
    ):
        main, tail = part[:MAIN].T, part[MAIN:].T
        ug_ref[rest, :MAIN] = main[: rest.stop - rest.start]
        ug_ref[rest, MAIN:] = tail[: rest.stop - rest.start]
    ug_out[:SHARE, :] = ug_ref[:, :MAIN]
    ug_out[SHARE:, :] = by_quarter([ug_ref[g * QUARTER : (g + 1) * QUARTER, MAIN:] for g in range(4)])
    column_ref[...] = x_ref[: MAIN + TAIL, :]


def partial(piece, start, x, out):
    found = dot_nt(piece[start : start + SHARE, :], x)
    out[:SHARE, :] = found[:, :MAIN].astype(BF)
    tail = [found[g * QUARTER : (g + 1) * QUARTER, MAIN:] for g in range(4)]
    out[SHARE:, :] = by_quarter(tail).astype(BF)


def near_kernel(x_ref, *refs):
    pieces, (out_ref, side_ref) = refs[:6], refs[6:]
    x = x_ref[...]
    for n, piece in enumerate(pieces):
        partial(piece, SIDE if n % 2 == 0 else 0, x, out_ref.at[n])
        if n % 2 == 0:
            side_ref[n // 2] = piece[:SIDE, :HID]


def pre_kernel(place, x_ref, near_ref, near_side, top_ref, bottom_ref, out_ref, side_ref):
    x = x_ref[...]
    far = (place[1] + 2) % NX
    partial(top_ref, SIDE, x, out_ref.at[2 * far])
    partial(bottom_ref, 0, x, out_ref.at[2 * far + 1])
    side_ref[far] = top_ref[:SIDE, :HID].astype(F32)
    for n, step in enumerate((0, 1, 3)):
        source = (place[1] + step) % NX
        out_ref[2 * source] = near_ref[2 * n]
        out_ref[2 * source + 1] = near_ref[2 * n + 1]
        side_ref[source] = near_side[n].astype(F32)


def gelu_slope(values):
    inner_arg = 0.7978845608 * (values + 0.044715 * values * values * values)
    tangent = jnp.tanh(inner_arg)
    return 0.5 * (1.0 + tangent) + 0.5 * values * (1.0 - tangent * tangent) * 0.7978845608 * (
        1.0 + 3.0 * 0.044715 * values * values
    )


def grad_kernel(place, parts_ref, ug_ref, side_ref, counts_ref, out_ref, sums_ref):
    tensor, x_me = place[0], place[1]
    side = side_ref[tensor // 2]
    bias = side[1:2] + side[2:3] + side[3:4]
    wanted = iota((SHARE, HID), 1) == (tensor % 2) * SHARE + iota((SHARE, HID), 0)
    bias = jnp.sum(jnp.where(wanted, bias, 0.0), axis=1, keepdims=True)
    counts = jnp.broadcast_to(counts_ref[...].astype(F32), (8, DP)).astype(BF)
    s = iota((DP, 128), 0)
    lane = iota((DP, 128), 1)
    many = dot(counts, onehot(s == lane // 8 * NX + x_me))[0:1]
    few = dot(counts, onehot(s == lane % TAIL // 2 * NX + x_me))[0:1]
    lane = iota((1, 128), 1)
    many = (lane % 8).astype(F32) < many
    few = (8 + lane % 2).astype(F32) < few
    pre = parts_ref[0].astype(F32)
    for j in range(1, NT):
        pre = pre + parts_ref[j].astype(F32)
    tail_bias = by_quarter([bias[g * QUARTER : (g + 1) * QUARTER] for g in range(4)])
    main = jnp.where(many, ug_ref[:SHARE] * gelu_slope(pre[:SHARE] + bias), 0.0)
    tail = jnp.where(few, ug_ref[SHARE:] * gelu_slope(pre[SHARE:] + tail_bias), 0.0)
    out_ref[:SHARE, :] = main.astype(BF)
    out_ref[SHARE:PACK, :] = tail.astype(BF)
    lane = iota((QUARTER, 128), 1) // 32
    total = jnp.sum(main, axis=1, keepdims=True) + jnp.concatenate(
        [jnp.sum(jnp.where(lane == g, tail, 0.0), axis=1, keepdims=True) for g in range(4)], axis=0
    )
    sums_ref[...] = sum_rows(total)


def unpacked(tail):
    lane = iota((QUARTER, 128), 1) // 32
    zero = jnp.zeros((), BF)
    return jnp.concatenate([jnp.where(lane == g, tail, zero) for g in range(4)], axis=0)


def moved_kernel(place, low_ref, other_ref, sums_ref, side_ref, out_ref):
    tensor, x_me = place[0], place[1]
    m = tensor % 2
    blocks = HID // BR
    owner = side_ref[tensor // 2][0:1, :blocks]
    r, c = iota((blocks, blocks), 0), iota((blocks, blocks), 1)
    column = jnp.sum(jnp.where(r == c, owner, 0.0), axis=1, keepdims=True)
    rank = jnp.sum(jnp.where((column == owner) & (r < c), 1.0, 0.0), axis=0, keepdims=True)
    target = jnp.broadcast_to(owner * MOST + rank, (8, blocks)).astype(BF)
    block, unit = iota((blocks, HID), 0), iota((blocks, HID), 1)
    within = unit - block * BR
    member = (within >= 0) & (within < BR)
    offset = jnp.sum(jnp.where(member, within, 0).astype(F32), axis=0, keepdims=True)
    key = dot(target, onehot(member))[0:1] * BR + offset
    low, other = low_ref[...], other_ref[...]
    both = [jnp.where(m == 0, low, other), jnp.where(m == 0, other, low)]
    main = jnp.concatenate([g[:SHARE] for g in both], axis=0)
    tail = jnp.concatenate([unpacked(g[SHARE:PACK]) for g in both], axis=0)
    r, c = iota((128, 128), 0), iota((128, 128), 1)
    tail = dot(tail, onehot((r % TAIL == c) & (c < TAIL))).astype(BF)
    rho = iota((DP * 8, 1), 0)
    dest, row = rho // 8, rho % 8
    wanted = (dest * MOST + m) * BR + row
    wanted = jnp.where(row < BR, wanted, -1).astype(F32)
    found = dot(onehot(wanted == key), jnp.concatenate([main, tail], axis=1))
    sums = sums_ref[...].astype(F32)
    for e in range(DP):
        here = found[e * 8 : (e + 1) * 8]
        here = jnp.concatenate([here[:, :128], here[:, 128:]], axis=0) + sums
        out_ref[e * 16 : (e + 1) * 16, :] = here.astype(BF)


def out_kernel(place, g_ref, *refs):
    pieces, (px_ref, full) = refs[: 2 * NX], refs[2 * NX :]
    for n in range(2 * NX):
        j = (place[1] + n // 2) % NX * 2 + n % 2
        full[n * SHARE : (n + 1) * SHARE, :MAIN] = g_ref[j, :SHARE, :]
        full[n * SHARE : (n + 1) * SHARE, MAIN:] = unpacked(g_ref[j, SHARE:PACK, :])
    g = full[...]
    here = [dot_nt(selector(i, True), g).astype(BF) for i in range(3)]
    total = [jnp.zeros((RHO, HALF), F32), jnp.zeros((RHO, HALF), F32)]
    for n, piece in enumerate(pieces):
        span = slice(n * SHARE, (n + 1) * SHARE)
        start = SIDE if n % 2 == 0 else 0
        last = piece[start:, 2 * HALF :]
        for side in range(2):
            part = dot(here[0][:, span], piece[start:, side * HALF : (side + 1) * HALF])
            total[side] = total[side] + part + dot(here[1 + side][:, span], last)
    for side in range(2):
        px_ref[:, side * HALF : (side + 1) * HALF] = total[side].astype(BF)


def order_kernel(place, _, in_ref, out_ref, block):
    n = BR * NZ
    r, c = iota((2 * n, RHO), 0), iota((2 * n, RHO), 1)
    row = r // NZ
    pick = onehot((c // 16 == r % NZ) & (c % 16 == jnp.where(row < BR, row, row + 8 - BR)))
    r, c = iota((128, 128), 0), iota((128, 128), 1)
    tail = jnp.zeros((n, 128), F32)
    sums = jnp.zeros((16, 128), F32)
    for x in range(NX):
        for z in range(NZ):
            block[z * 16 : (z + 1) * 16, :] = in_ref[z * NX + x]
        found = dot(pick, block[...]).astype(BF)
        out_ref[x * n : (x + 1) * n, :] = found[:n]
        tail = tail + dot(found[n:], onehot((r < TAIL) & (c == r + x * TAIL)))
        sums = sums + in_ref[place[2] * NX + x].astype(F32)
    out_ref[NX * n : MOVED * NZ, :] = tail.astype(BF)
    row = iota((8, 128), 0)
    for i, (a, b, c) in enumerate(((6, 7, 14), (8, 9, 10))):
        total = sums[c : c + 1] + sums[b : b + 1] + sums[a : a + 1]
        high, mid, low = pieces_of(total)
        part = jnp.where(row == 0, high, jnp.where(row == 1, mid, jnp.where(row == 2, low, 0.0)))
        parts = part if i == 0 else jnp.concatenate([parts, part], axis=0)
    out_ref[MOVED * NZ :, :] = parts.astype(BF)


def slots_kernel(in_ref, out_ref):
    total = in_ref[0].astype(F32)
    for z in range(1, NZ):
        total = total + in_ref[z].astype(F32)
    total = total.astype(BF)
    left, right = total[:, :HALF], total[:, HALF:]
    r, c = iota((16, 16), 0), iota((16, 16), 1)
    halfway = (c - SLOTS) * 2
    last = dot(onehot(r == halfway), left) + dot(onehot(r == halfway + 1), right)
    out_ref[:, : 2 * HALF] = total[:SLOTS]
    out_ref[:, 2 * HALF :] = last[:SLOTS].astype(BF)


def weight_kernel(place, m_ref, *refs):
    columns, (out_ref, bias_ref, found, tails) = refs[:NX], refs[NX:]
    lane, unit = iota((128, HID), 0), iota((128, HID), 1)
    row = iota((16, 128), 0)
    total = jnp.zeros((16, HID), F32)
    for h in range(2):
        sums = m_ref[place[1] * 2 + h, MOVED * NZ :, :]
        for i in range(2):
            mine = (unit == h * SHARE + i * 64 + lane) & (lane >= i * 64)
            total = total + dot(jnp.where(row // 8 == i, sums, jnp.zeros((), BF)), onehot(mine))
    total = total[:8] + total[8:]
    bias_ref[...] = (total[2:3] + total[1:2] + total[0:1]).reshape(HID)
    n = BR * NZ
    for j in range(NT):
        for k in range(NX + 1):
            start = pl.multiple_of((place[1] + k) % NX * n, n) if k < NX else NX * n
            block = m_ref[j, pl.ds(start, n), :]
            for b in range(BR):
                row = b * MOST * DP + j * NZ
                found[row : row + NZ, k * 128 : (k + 1) * 128] = block[b * NZ : (b + 1) * NZ]
    r, c = iota((MOST * DP, MOST * DP), 0), iota((MOST * DP, MOST * DP), 1)
    order = onehot(c == r % NT * NZ + r // NT)
    for k in range(NX):
        tails[(place[1] + k) % NX] = columns[k][MAIN:, :]
    tail = tails[...].reshape(NX * TAIL, 3 * HALF)
    for b in range(BR):
        mine = dot(order, found[b * MOST * DP : (b + 1) * MOST * DP, :]).astype(BF)
        total = dot(mine[:, NX * 128 :], tail)
        for k in range(NX):
            total = total + dot(mine[:, k * 128 : (k + 1) * 128], columns[k][:MAIN, :])
        out_ref[b] = total.astype(BF)


def arrived_kernel(*refs):
    refs[-1][...] = jnp.zeros_like(refs[-1])


def arrived(arrays):
    return pl.pallas_call(
        arrived_kernel,
        out_shape=jax.ShapeDtypeStruct((8, 128), F32),
        in_specs=[pl.BlockSpec(memory_space=ANY)] * len(arrays),
        out_specs=pl.BlockSpec(memory_space=VMEM),
        cost_estimate=pl.CostEstimate(flops=50 * 10**9, bytes_accessed=0, transcendentals=0),
    )(*arrays)


def to_left(value):
    return lax.ppermute(value, "x", [(i, (i - 1) % NX) for i in range(NX)])


def to_right(value):
    return lax.ppermute(value, "x", [(i, (i + 1) % NX) for i in range(NX)])


def across(value):
    return lax.ppermute(value, "x", [(i, (i + 2) % NX) for i in range(NX)])


def body(x_slots, counts, w, bias, upstream, owners):
    tensor = lax.axis_index(("y", "core")).astype(I32)
    x_me = lax.axis_index("x").astype(I32)
    place = jnp.stack([tensor, x_me, lax.axis_index("z").astype(I32)])
    top, bottom, packed = call(
        pack_kernel,
        [((FIRST, 3 * HALF), BF), ((SHARE, 3 * HALF), BF), ((NZ, 16, WIDTH), BF)],
        [place, x_slots, upstream, w, bias, owners.reshape(1, DP)],
        1,
        [
            VMEM((SLOTS, 3 * HALF), BF),
            VMEM((SLOTS, NZ * GROUP), BF),
            VMEM((HID,), F32),
            VMEM((1, DP), I32),
            VMEM((16, 3 * HALF), BF),
            VMEM((RHO, 256), BF),
            pltpu.SemaphoreType.DMA((6,)),
        ],
        2 * RHO * GROUP * 256,
        5 * 10**6,
        (1, 2, 3, 4, 5),
        HBM,
        LARGE,
    )
    next_top, prev_bottom = to_left(top), to_right(bottom)
    along_z = lax.all_to_all(packed, "z", 0, 0, tiled=True)
    there = arrived([next_top, prev_bottom])
    top, bottom, next_top, prev_bottom, there = lax.optimization_barrier((top, bottom, next_top, prev_bottom, there))
    far_top, far_bottom = to_left(next_top), to_right(prev_bottom)
    next_bottom, prev_top = to_left(bottom), to_right(top)
    pieces = [top, bottom, next_top, next_bottom, far_top, far_bottom, prev_top, prev_bottom]
    rows, column, ug = call(
        rows_kernel,
        [((256, 3 * HALF), BF), ((MAIN + TAIL, 3 * HALF), BF), ((PACK, 128), F32)],
        [there, along_z.reshape(RHO, WIDTH)],
        0,
        [VMEM((SHARE, 256), F32)],
        flops=2 * 256 * 256 * 9 * 256,
        moved=2 * 10**6,
    )
    near, near_side = call(
        near_kernel,
        [((6, PACK, 128), BF), ((3, SIDE, HID), BF)],
        [rows] + pieces[:4] + pieces[6:],
        flops=2 * GROUP * 256 * 3 * HALF,
        moved=4 * 10**6,
    )
    part, side = call(
        pre_kernel,
        [((NT, PACK, 128), BF), ((NX, SIDE, HID), F32)],
        [place, rows, near, near_side] + pieces[4:6],
        1,
        flops=GROUP * 256 * HALF,
        moved=2 * 10**6,
    )
    columns = [column, to_left(column), across(column), to_right(column)]
    there = arrived(columns[1::2])
    parts = lax.all_to_all(part, ("y", "core"), 0, 0, tiled=True)
    low, sums = call(
        grad_kernel,
        [((PACK, 128), BF), ((16, 128), BF)],
        [place, parts, ug, side, counts.reshape(1, DP)],
        1,
        moved=10**6,
    )
    other = lax.ppermute(low, "core", [(0, 1), (1, 0)])
    sent, = call(
        moved_kernel,
        [((DP * 16, 128), BF)],
        [place, low, other, sums, side],
        1,
        flops=2 * 8 * 96 * HID * 128,
        moved=10**6,
    )
    moved = lax.all_to_all(sent.reshape(DP, 16, 128), ("z", "x"), 0, 0, tiled=True)
    low, sent = lax.optimization_barrier((low, sent))
    grad = lax.all_gather(low, ("y", "core"), axis=0)
    px, = call(
        out_kernel,
        [((RHO, 2 * HALF), BF)],
        [place, grad] + pieces,
        1,
        [VMEM((GROUP, 256), BF)],
        2 * RHO * GROUP * (4 * HALF + 3 * 256),
        6 * 10**6,
    )
    px, moved, there = lax.optimization_barrier((px, moved, there))
    pz = lax.all_to_all(px.reshape(NZ, 16, 2 * HALF), "z", 0, 0, tiled=True)
    moved, = call(
        order_kernel,
        [((MOVED * NZ + 16, 128), BF)],
        [place, there, moved],
        1,
        [VMEM((RHO, 128), BF)],
        moved=10**6,
    )
    moved = lax.all_gather(moved, ("y", "core"), axis=0)
    found, grad_bias = call(
        weight_kernel,
        [((BR, MOST * DP, 3 * HALF), BF), ((HID,), F32)],
        [place, moved] + columns,
        1,
        [VMEM((NT * BR * NZ, 640), BF), VMEM((NX, TAIL, 3 * HALF), BF)],
        2 * 768 * 640 * 1536,
        5 * 10**6,
    )
    grad_slots, = call(slots_kernel, [((SLOTS, 3 * HALF), BF)], [pz], moved=10**6)
    return grad_slots, grad_bias, found.transpose(1, 0, 2)


def solution(mesh):
    fine = Mesh(mesh.devices.reshape(NZ, NX, NT // 2, 2), ("z", "x", "y", "core"))
    rows, cols = ("z", "x"), ("y", "core")
    in_specs = (P(rows, cols), P(), P(rows, cols), P(rows), P(rows, None), P(rows, None))
    out_specs = (P(rows, cols), P(rows), P(rows, None, cols))
    return jax.shard_map(body, mesh=fine, in_specs=in_specs, out_specs=out_specs, check_vma=False)
```

```python
import functools

import jax
import jax.numpy as jnp
from jax import lax
from jax.experimental import pallas as pl
from jax.experimental.pallas import tpu as pltpu
from jax.sharding import Mesh, PartitionSpec as P

BF, F32, I32 = jnp.bfloat16, jnp.float32, jnp.int32
MOST = 2
BR = 6
SLOTS = 10
HALF = 512
NZ, NX, NT = 16, 4, 8
DP = NZ * NX
HID = 384
GROUP = NX * HID
SHARE = GROUP // NT
QUARTER = SHARE // 4
MAIN, TAIL = NZ * 8, NZ * 2
RHO = NZ * 16
PACK = SHARE + QUARTER
SIDE = 16
FIRST = SIDE + SHARE
FULL = SIDE + HID
MOVED = (NX + 1) * BR
LIMIT = 16 * 1024 * 1024
LARGE = 56 * 1024 * 1024
WIDTH = 2 * HALF + 128
TILES = 3 * HALF // 128
ROWS = SLOTS * TILES


def iota(shape, dim):
    return lax.broadcasted_iota(I32, shape, dim)


def onehot(mask):
    return jnp.where(mask, 1.0, 0.0).astype(BF)


def dot(a, b):
    return jnp.dot(a, b, preferred_element_type=F32)


def dot_nt(a, b):
    return lax.dot_general(a, b, (((1,), (1,)), ((), ())), preferred_element_type=F32)


VMEM, HBM, ANY, SMEM = pltpu.VMEM, pltpu.HBM, pl.ANY, pltpu.SMEM


def call(kernel, outs, args, scalars=0, scratch=(), flops=0, moved=0, outside=(), space=ANY, limit=LIMIT):
    specs = [
        pl.BlockSpec(memory_space=SMEM if i < scalars else space if i in outside else VMEM)
        for i in range(len(args))
    ]
    return pl.pallas_call(
        kernel,
        out_shape=[jax.ShapeDtypeStruct(s, d) for s, d in outs],
        in_specs=specs,
        out_specs=[pl.BlockSpec(memory_space=VMEM)] * len(outs),
        scratch_shapes=list(scratch),
        compiler_params=pltpu.CompilerParams(vmem_limit_bytes=limit),
        cost_estimate=pl.CostEstimate(flops=flops, bytes_accessed=moved, transcendentals=0),
    )(*args)


def pieces_of(value):
    high = value.astype(BF).astype(F32)
    mid = (value - high).astype(BF).astype(F32)
    return high, mid, value - high - mid


def pack_kernel(place, x_in, up_in, w_in, bias_in, owner_in, top_ref, bottom_ref, out_ref, x_ref, up_ref, bias_ref, owner_ref, rows, ups, sems):
    copies = [
        pltpu.make_async_copy(source, target, sems.at[i])
        for i, (source, target) in enumerate(
            [
                (up_in, up_ref),
                (x_in, x_ref),
                (bias_in, bias_ref),
                (owner_in, owner_ref),
                (w_in.at[pl.ds(0, SHARE), :], top_ref.at[pl.ds(SIDE, SHARE), :]),
                (w_in.at[pl.ds(SHARE, SHARE), :], bottom_ref),
            ]
        )
    ]
    for copy in copies:
        copy.start()
    skip = place[0] % 2 * 64
    k, lane = iota((256, 384), 0) - skip, iota((256, 384), 1)
    pick = (lane < 128) & (k == lane)
    pick = pick | ((lane >= 128) & (lane < 192) & (k == lane))
    pick = onehot(pick | ((lane >= 320) & (k == lane - 192)))
    k, lane = iota((RHO, RHO), 0), iota((RHO, RHO), 1)
    block = k // 16 == lane // 16
    k, lane = k % 16, lane % 16
    kept = onehot(block & (k == lane) & (k < SLOTS))
    kept_even = onehot(block & (lane == 2 * (k - SLOTS)))
    kept_odd = onehot(block & (lane == 2 * (k - SLOTS) + 1))
    r, c = iota((16, 16), 0), iota((16, 16), 1)
    same = onehot((r == c) & (r < SLOTS))
    even = onehot(c == 2 * (r - SLOTS))
    odd = onehot(c == 2 * (r - SLOTS) + 1)
    rows[...] = jnp.zeros_like(rows)
    ups[...] = jnp.zeros_like(ups)
    copies[0].wait()
    for z in range(NZ):
        start = pl.multiple_of(z * GROUP + place[0] * 3 // 2 * 128, 128)
        ups[z * 16 : z * 16 + SLOTS, :] = up_ref[:, pl.ds(start, 256)]
    chosen = dot(ups[...], pick).astype(BF)
    chosen = dot(kept, chosen[:, :128]) + dot(kept_even, chosen[:, 128:256]) + dot(kept_odd, chosen[:, 256:])
    chosen = chosen.astype(BF)
    copies[1].wait()
    rows[0:SLOTS, :] = x_ref[...]
    a, b, last = rows[:, :HALF], rows[:, HALF : 2 * HALF], rows[:, 2 * HALF :]
    left = (dot(same, a) + dot(even, last)).astype(BF)
    right = (dot(same, b) + dot(odd, last)).astype(BF)
    for z in range(NZ):
        out_ref[z, :, :HALF] = left
        out_ref[z, :, HALF : 2 * HALF] = right
        out_ref[z, :, 2 * HALF :] = chosen[z * 16 : z * 16 + 16]
    copies[2].wait()
    row = iota((SIDE, HID), 0)
    high, mid, low = pieces_of(bias_ref[...].reshape(1, HID))
    side = jnp.where(row == 1, high, jnp.where(row == 2, mid, jnp.where(row == 3, low, 0.0)))
    copies[3].wait()
    owner = jnp.where(iota((SIDE, DP), 0) == 0, owner_ref[...].astype(F32), 0.0).astype(BF)
    owner = dot(owner, onehot(iota((DP, HID), 0) == iota((DP, HID), 1)))
    top_ref[:SIDE, :HID] = (owner + side).astype(BF)
    top_ref[:SIDE, HID:] = jnp.zeros((SIDE, 3 * HALF - HID), BF)
    copies[4].wait()
    copies[5].wait()


def sum_rows(total):
    high, mid, low = pieces_of(total)
    lane = iota((SHARE, 128), 1)
    pieces = jnp.where(lane == 0, high, jnp.where(lane == 1, mid, jnp.where(lane == 2, low, 0.0)))
    pieces = jnp.concatenate([pieces, jnp.zeros((256 - SHARE, 128), F32)], axis=0).T[:16].astype(BF)
    r, c = iota((16, 16), 0), iota((16, 16), 1)
    shift = onehot(iota((128, 128), 0) + 64 == iota((128, 128), 1))
    rest = dot(pieces[:, 128:], shift).astype(BF)
    head = (c < 3) & (r == jnp.where(c < 2, c + 6, 14))
    rows = dot(onehot(head), pieces[:, :128]) + dot(onehot((r == c + 8) & (c < 3)), rest)
    return rows.astype(BF)


def slot_of(i):
    tail = (i - MAIN) % TAIL
    return jnp.where(i < MAIN, i // 8, tail // 2), jnp.where(i < MAIN, i % 8, 8 + tail % 2)


def selector(third):
    i, rho = iota((256, RHO), 0), iota((256, RHO), 1)
    z, slot = slot_of(i)
    if third == 0:
        return onehot(rho == z * 16 + slot)
    return onehot((rho == z * 16 + SLOTS + slot // 2) & (slot % 2 == third - 1))


def by_quarter(pieces):
    lane = iota((QUARTER, 128), 1) // 32
    found = jnp.where(lane == 0, pieces[0], 0.0)
    for g in range(1, 4):
        found = jnp.where(lane == g, pieces[g], found)
    return found


def select_rows(rz_ref, x_ref, column_ref):
    left, right = rz_ref[:, :HALF], rz_ref[:, HALF : 2 * HALF]
    first = selector(0)
    x_ref[:, :HALF] = dot(first, left).astype(BF)
    x_ref[:, HALF : 2 * HALF] = dot(first, right).astype(BF)
    x_ref[:, 2 * HALF :] = (dot(selector(1), left) + dot(selector(2), right)).astype(BF)
    column_ref[...] = x_ref[: MAIN + TAIL, :]


def ups_kernel(rz_ref, ug_ref, held):
    ups = rz_ref[:, 2 * HALF :]
    r, c = iota((128, 128), 0), iota((128, 128), 1)
    low, high = dot(ups, onehot((r == c) & (r < 64))).astype(BF), dot(ups, onehot(r == c + 64)).astype(BF)
    for part, rest in (
        (dot(selector(0), ups), slice(0, 128)),
        (dot(selector(1), low) + dot(selector(2), high), slice(128, SHARE)),
    ):
        main, tail = part[:MAIN].T, part[MAIN:].T
        held[rest, :MAIN] = main[: rest.stop - rest.start]
        held[rest, MAIN:] = tail[: rest.stop - rest.start]
    ug_ref[:SHARE, :] = held[:, :MAIN]
    ug_ref[SHARE:, :] = by_quarter([held[g * QUARTER : (g + 1) * QUARTER, MAIN:] for g in range(4)])


def partial(piece, start, x, out):
    found = dot_nt(piece[start : start + SHARE, :], x)
    out[:SHARE, :] = found[:, :MAIN].astype(BF)
    tail = [found[g * QUARTER : (g + 1) * QUARTER, MAIN:] for g in range(4)]
    out[SHARE:, :] = by_quarter(tail).astype(BF)


def near_kernel(rz_ref, *refs):
    pieces, (x_ref, column_ref, out_ref, side_ref) = refs[:6], refs[6:]
    select_rows(rz_ref, x_ref, column_ref)
    x = x_ref[...]
    for n, piece in enumerate(pieces):
        partial(piece, SIDE if n % 2 == 0 else 0, x, out_ref.at[n])
        if n % 2 == 0:
            side_ref[n // 2] = piece[:SIDE, :HID]


def pre_kernel(place, x_ref, near_ref, near_side, top_ref, bottom_ref, out_ref, side_ref):
    x = x_ref[...]
    far = (place[1] + 2) % NX
    partial(top_ref, SIDE, x, out_ref.at[2 * far])
    partial(bottom_ref, 0, x, out_ref.at[2 * far + 1])
    side_ref[far] = top_ref[:SIDE, :HID].astype(F32)
    for n, step in enumerate((0, 1, 3)):
        source = (place[1] + step) % NX
        out_ref[2 * source] = near_ref[2 * n]
        out_ref[2 * source + 1] = near_ref[2 * n + 1]
        side_ref[source] = near_side[n].astype(F32)


def gelu_slope(values):
    inner_arg = 0.7978845608 * (values + 0.044715 * values * values * values)
    tangent = jnp.tanh(inner_arg)
    return 0.5 * (1.0 + tangent) + 0.5 * values * (1.0 - tangent * tangent) * 0.7978845608 * (
        1.0 + 3.0 * 0.044715 * values * values
    )


def grad_kernel(place, parts_ref, ug_ref, side_ref, counts_ref, out_ref, sums_ref):
    tensor, x_me = place[0], place[1]
    side = side_ref[tensor // 2]
    bias = side[1:2] + side[2:3] + side[3:4]
    wanted = iota((SHARE, HID), 1) == (tensor % 2) * SHARE + iota((SHARE, HID), 0)
    bias = jnp.sum(jnp.where(wanted, bias, 0.0), axis=1, keepdims=True)
    counts = jnp.broadcast_to(counts_ref[...].astype(F32), (8, DP)).astype(BF)
    s = iota((DP, 128), 0)
    lane = iota((DP, 128), 1)
    many = dot(counts, onehot(s == lane // 8 * NX + x_me))[0:1]
    few = dot(counts, onehot(s == lane % TAIL // 2 * NX + x_me))[0:1]
    lane = iota((1, 128), 1)
    many = (lane % 8).astype(F32) < many
    few = (8 + lane % 2).astype(F32) < few
    pre = parts_ref[0].astype(F32)
    for j in range(1, NT):
        pre = pre + parts_ref[j].astype(F32)
    tail_bias = by_quarter([bias[g * QUARTER : (g + 1) * QUARTER] for g in range(4)])
    main = jnp.where(many, ug_ref[:SHARE] * gelu_slope(pre[:SHARE] + bias), 0.0)
    tail = jnp.where(few, ug_ref[SHARE:] * gelu_slope(pre[SHARE:] + tail_bias), 0.0)
    out_ref[:SHARE, :] = main.astype(BF)
    out_ref[SHARE:PACK, :] = tail.astype(BF)
    lane = iota((QUARTER, 128), 1) // 32
    total = jnp.sum(main, axis=1, keepdims=True) + jnp.concatenate(
        [jnp.sum(jnp.where(lane == g, tail, 0.0), axis=1, keepdims=True) for g in range(4)], axis=0
    )
    sums_ref[...] = sum_rows(total)


def unpacked(tail):
    lane = iota((QUARTER, 128), 1) // 32
    zero = jnp.zeros((), BF)
    return jnp.concatenate([jnp.where(lane == g, tail, zero) for g in range(4)], axis=0)


def moved_kernel(place, low_ref, other_ref, sums_ref, side_ref, out_ref):
    tensor, x_me = place[0], place[1]
    m = tensor % 2
    blocks = HID // BR
    owner = side_ref[tensor // 2][0:1, :blocks]
    r, c = iota((blocks, blocks), 0), iota((blocks, blocks), 1)
    column = jnp.sum(jnp.where(r == c, owner, 0.0), axis=1, keepdims=True)
    rank = jnp.sum(jnp.where((column == owner) & (r < c), 1.0, 0.0), axis=0, keepdims=True)
    target = jnp.broadcast_to(owner * MOST + rank, (8, blocks)).astype(BF)
    block, unit = iota((blocks, HID), 0), iota((blocks, HID), 1)
    within = unit - block * BR
    member = (within >= 0) & (within < BR)
    offset = jnp.sum(jnp.where(member, within, 0).astype(F32), axis=0, keepdims=True)
    key = dot(target, onehot(member))[0:1] * BR + offset
    low, other = low_ref[...], other_ref[...]
    both = [jnp.where(m == 0, low, other), jnp.where(m == 0, other, low)]
    main = jnp.concatenate([g[:SHARE] for g in both], axis=0)
    tail = jnp.concatenate([unpacked(g[SHARE:PACK]) for g in both], axis=0)
    r, c = iota((128, 128), 0), iota((128, 128), 1)
    tail = dot(tail, onehot((r % TAIL == c) & (c < TAIL))).astype(BF)
    rho = iota((DP * 8, 1), 0)
    dest, row = rho // 8, rho % 8
    wanted = (dest * MOST + m) * BR + row
    wanted = jnp.where(row < BR, wanted, -1).astype(F32)
    found = dot(onehot(wanted == key), jnp.concatenate([main, tail], axis=1))
    sums = sums_ref[...].astype(F32)
    for e in range(DP):
        here = found[e * 8 : (e + 1) * 8]
        here = jnp.concatenate([here[:, :128], here[:, 128:]], axis=0) + sums
        out_ref[e * 16 : (e + 1) * 16, :] = here.astype(BF)


def out_kernel(place, g_ref, *refs):
    pieces, (px_ref, full) = refs[: 2 * NX], refs[2 * NX :]
    for n in range(2 * NX):
        j = (place[1] + n // 2) % NX * 2 + n % 2
        full[n * SHARE : (n + 1) * SHARE, :MAIN] = g_ref[j, :SHARE, :]
        full[n * SHARE : (n + 1) * SHARE, MAIN:] = unpacked(g_ref[j, SHARE:PACK, :])
    g = full[...]
    rho, lane = iota((2 * MAIN, 256), 0), iota((2 * MAIN, 256), 1)
    tail = (lane >= MAIN) & (lane % TAIL == (rho - MAIN) // 4)
    tail = tail & (rho >= MAIN)
    here = dot_nt(onehot(tail | ((lane == rho) & (rho < MAIN))), g).astype(BF)
    total = jnp.zeros((2 * MAIN, 3 * HALF), F32)
    for n, piece in enumerate(pieces):
        start = SIDE if n % 2 == 0 else 0
        total = total + dot(here[:, n * SHARE : (n + 1) * SHARE], piece[start:, :])
    tiles = [total[:MAIN, t * 128 : (t + 1) * 128] for t in range(TILES)]
    quarter = iota((MAIN, 128), 0) % 4
    for i in range(TILES // 4):
        tile = jnp.zeros((MAIN, 128), F32)
        for q in range(4):
            t = 4 * i + q
            tile = jnp.where(quarter == q, total[MAIN:, t * 128 : (t + 1) * 128], tile)
        tiles.append(tile)
    for z in range(NZ):
        blocks = [tile[z * 8 : (z + 1) * 8] for tile in tiles]
        for u in range(len(blocks) // 2):
            both = jnp.concatenate([blocks[2 * u], blocks[2 * u + 1]], axis=0)
            px_ref[z, u * 16 : (u + 1) * 16, :] = both.astype(BF)
        px_ref[z, ROWS - 8 :, :] = blocks[-1].astype(BF)


def order_kernel(place, in_ref, weights_there, columns_there, out_ref, block):
    del weights_there, columns_there
    n = BR * NZ
    r, c = iota((2 * n, RHO), 0), iota((2 * n, RHO), 1)
    row = r // NZ
    pick = onehot((c // 16 == r % NZ) & (c % 16 == jnp.where(row < BR, row, row + 8 - BR)))
    r, c = iota((128, 128), 0), iota((128, 128), 1)
    tail = jnp.zeros((n, 128), F32)
    sums = jnp.zeros((16, 128), F32)
    for x in range(NX):
        for z in range(NZ):
            block[z * 16 : (z + 1) * 16, :] = in_ref[z * NX + x]
        found = dot(pick, block[...]).astype(BF)
        out_ref[x * n : (x + 1) * n, :] = found[:n]
        tail = tail + dot(found[n:], onehot((r < TAIL) & (c == r + x * TAIL)))
        sums = sums + in_ref[place[2] * NX + x].astype(F32)
    out_ref[NX * n : MOVED * NZ, :] = tail.astype(BF)
    row = iota((8, 128), 0)
    for i, (a, b, c) in enumerate(((6, 7, 14), (8, 9, 10))):
        total = sums[c : c + 1] + sums[b : b + 1] + sums[a : a + 1]
        high, mid, low = pieces_of(total)
        part = jnp.where(row == 0, high, jnp.where(row == 1, mid, jnp.where(row == 2, low, 0.0)))
        parts = part if i == 0 else jnp.concatenate([parts, part], axis=0)
    out_ref[MOVED * NZ :, :] = parts.astype(BF)


def slots_kernel(in_ref, out_ref, held):
    total = in_ref[0].astype(F32)
    for z in range(1, NZ):
        total = total + in_ref[z].astype(F32)
    for t in range(TILES):
        span = slice(t * 128, (t + 1) * 128)
        held[:8, span] = total[t * 8 : (t + 1) * 8]
        for s in range(2):
            row = 8 * TILES + t // 4 * 8 + s * 4 + t % 4
            held[8 + s : 9 + s, span] = total[row : row + 1]
    out_ref[...] = held[:SLOTS, :].astype(BF)


def weight_kernel(place, m_ref, *refs):
    columns, (out_ref, bias_ref, found, held) = refs[:NX], refs[NX:]
    lane, unit = iota((128, HID), 0), iota((128, HID), 1)
    row = iota((16, 128), 0)
    total = jnp.zeros((16, HID), F32)
    for h in range(2):
        sums = m_ref[place[1] * 2 + h, MOVED * NZ :, :]
        for i in range(2):
            mine = (unit == h * SHARE + i * 64 + lane) & (lane >= i * 64)
            total = total + dot(jnp.where(row // 8 == i, sums, jnp.zeros((), BF)), onehot(mine))
    total = total[:8] + total[8:]
    bias_ref[...] = (total[2:3] + total[1:2] + total[0:1]).reshape(HID)
    n = BR * NZ
    for j in range(NT):
        for k in range(NX + 1):
            start = pl.multiple_of((place[1] + k) % NX * n, n) if k < NX else NX * n
            block = m_ref[j, pl.ds(start, n), :]
            for b in range(BR):
                row = b * MOST * DP + j * NZ
                found[row : row + NZ, k * 128 : (k + 1) * 128] = block[b * NZ : (b + 1) * NZ]
    r, c = iota((MOST * DP, MOST * DP), 0), iota((MOST * DP, MOST * DP), 1)
    order = onehot(c == r % NT * NZ + r // NT)
    for k, column in enumerate(columns):
        held[k * MAIN : (k + 1) * MAIN, :] = column[:MAIN, :]
        start = pl.multiple_of(NX * MAIN + (place[1] + k) % NX * TAIL, TAIL)
        held[pl.ds(start, TAIL), :] = column[MAIN:, :]
    for b in range(BR):
        span = slice(b * MOST * DP, (b + 1) * MOST * DP)
        found[span, :] = dot(order, found[span, :]).astype(BF)
    for third in range(3):
        span = slice(third * HALF, (third + 1) * HALF)
        total = dot(found[...], held[:, span]).astype(BF)
        for b in range(BR):
            out_ref[b, :, span] = total[b * MOST * DP : (b + 1) * MOST * DP]


def arrived_kernel(*refs):
    refs[-1][...] = jnp.zeros_like(refs[-1])


def arrived(arrays):
    return pl.pallas_call(
        arrived_kernel,
        out_shape=jax.ShapeDtypeStruct((8, 128), F32),
        in_specs=[pl.BlockSpec(memory_space=ANY)] * len(arrays),
        out_specs=pl.BlockSpec(memory_space=VMEM),
        cost_estimate=pl.CostEstimate(flops=50 * 10**9, bytes_accessed=0, transcendentals=0),
    )(*arrays)


def to_left(value):
    return lax.ppermute(value, "x", [(i, (i - 1) % NX) for i in range(NX)])


def to_right(value):
    return lax.ppermute(value, "x", [(i, (i + 1) % NX) for i in range(NX)])


def across(value):
    return lax.ppermute(value, "x", [(i, (i + 2) % NX) for i in range(NX)])


def body(x_slots, counts, w, bias, upstream, owners):
    tensor = lax.axis_index(("y", "core")).astype(I32)
    x_me = lax.axis_index("x").astype(I32)
    place = jnp.stack([tensor, x_me, lax.axis_index("z").astype(I32)])
    top, bottom, packed = call(
        pack_kernel,
        [((FIRST, 3 * HALF), BF), ((SHARE, 3 * HALF), BF), ((NZ, 16, WIDTH), BF)],
        [place, x_slots, upstream, w, bias, owners.reshape(1, DP)],
        1,
        [
            VMEM((SLOTS, 3 * HALF), BF),
            VMEM((SLOTS, NZ * GROUP), BF),
            VMEM((HID,), F32),
            VMEM((1, DP), I32),
            VMEM((16, 3 * HALF), BF),
            VMEM((RHO, 256), BF),
            pltpu.SemaphoreType.DMA((6,)),
        ],
        2 * RHO * GROUP * 256,
        5 * 10**6,
        (1, 2, 3, 4, 5),
        HBM,
        LARGE,
    )
    next_top, prev_bottom = to_left(top), to_right(bottom)
    along_z = lax.all_to_all(packed, "z", 0, 0, tiled=True)
    there = arrived([next_top, prev_bottom])
    top, bottom, next_top, prev_bottom, there = lax.optimization_barrier((top, bottom, next_top, prev_bottom, there))
    far_top, far_bottom = to_left(next_top), to_right(prev_bottom)
    next_bottom, prev_top = to_left(bottom), to_right(top)
    pieces = [top, bottom, next_top, next_bottom, far_top, far_bottom, prev_top, prev_bottom]
    rows, column, near, near_side = call(
        near_kernel,
        [((256, 3 * HALF), BF), ((MAIN + TAIL, 3 * HALF), BF), ((6, PACK, 128), BF), ((3, SIDE, HID), BF)],
        [along_z.reshape(RHO, WIDTH)] + pieces[:4] + pieces[6:],
        flops=2 * GROUP * 256 * 3 * HALF,
        moved=4 * 10**6,
    )
    part, side = call(
        pre_kernel,
        [((NT, PACK, 128), BF), ((NX, SIDE, HID), F32)],
        [place, rows, near, near_side] + pieces[4:6],
        1,
        flops=GROUP * 256 * HALF,
        moved=2 * 10**6,
    )
    part, along_z = lax.optimization_barrier((part, along_z))
    ug, = call(
        ups_kernel,
        [((PACK, 128), F32)],
        [along_z.reshape(RHO, WIDTH)],
        0,
        [VMEM((SHARE, 256), F32)],
        flops=10**9,
        moved=10**6,
    )
    columns = [column, to_left(column), across(column), to_right(column)]
    columns_there = arrived(columns[1::2])
    parts = lax.all_to_all(part, ("y", "core"), 0, 0, tiled=True)
    low, sums = call(
        grad_kernel,
        [((PACK, 128), BF), ((16, 128), BF)],
        [place, parts, ug, side, counts.reshape(1, DP)],
        1,
        moved=10**6,
    )
    other = lax.ppermute(low, "core", [(0, 1), (1, 0)])
    sent, = call(
        moved_kernel,
        [((DP * 16, 128), BF)],
        [place, low, other, sums, side],
        1,
        flops=2 * 8 * 96 * HID * 128,
        moved=10**6,
    )
    moved = lax.all_to_all(sent.reshape(DP, 16, 128), ("z", "x"), 0, 0, tiled=True)
    low, sent = lax.optimization_barrier((low, sent))
    grad = lax.all_gather(low, ("y", "core"), axis=0)
    px, = call(
        out_kernel,
        [((NZ, ROWS, 128), BF)],
        [place, grad] + pieces,
        1,
        [VMEM((GROUP, 256), BF)],
        2 * RHO * GROUP * (4 * HALF + 3 * 256),
        6 * 10**6,
    )
    px, moved, columns_there = lax.optimization_barrier((px, moved, columns_there))
    pz = lax.all_to_all(px, "z", 0, 0, tiled=True)
    moved, = call(
        order_kernel,
        [((MOVED * NZ + 16, 128), BF)],
        [place, moved, there, columns_there],
        1,
        [VMEM((RHO, 128), BF)],
        moved=10**6,
    )
    moved = lax.all_gather(moved, ("y", "core"), axis=0)
    found, grad_bias = call(
        weight_kernel,
        [((BR, MOST * DP, 3 * HALF), BF), ((HID,), F32)],
        [place, moved] + columns,
        1,
        [VMEM((NT * BR * NZ, 640), BF), VMEM((NX * (MAIN + TAIL), 3 * HALF), BF)],
        2 * 768 * 640 * 1536,
        5 * 10**6,
    )
    grad_slots, = call(
        slots_kernel, [((SLOTS, 3 * HALF), BF)], [pz], 0, [VMEM((16, 3 * HALF), F32)], moved=10**6
    )
    return grad_slots, grad_bias, found.transpose(1, 0, 2)


def solution(mesh):
    fine = Mesh(mesh.devices.reshape(NZ, NX, NT // 2, 2), ("z", "x", "y", "core"))
    rows, cols = ("z", "x"), ("y", "core")
    in_specs = (P(rows, cols), P(), P(rows, cols), P(rows), P(rows, None), P(rows, None))
    out_specs = (P(rows, cols), P(rows), P(rows, None, cols))
    return jax.shard_map(body, mesh=fine, in_specs=in_specs, out_specs=out_specs, check_vma=False)
```

```python
import functools

import jax
import jax.numpy as jnp
from jax import lax
from jax.experimental import pallas as pl
from jax.experimental.pallas import tpu as pltpu
from jax.sharding import Mesh, PartitionSpec as P

BF, F32, I32 = jnp.bfloat16, jnp.float32, jnp.int32
MOST = 2
BR = 6
SLOTS = 10
HALF = 512
NZ, NX, NT = 16, 4, 8
DP = NZ * NX
HID = 384
GROUP = NX * HID
SHARE = GROUP // NT
QUARTER = SHARE // 4
MAIN, TAIL = NZ * 8, NZ * 2
RHO = NZ * 16
PACK = SHARE + QUARTER
SIDE = 16
FIRST = SIDE + SHARE
FULL = SIDE + HID
MOVED = (NX + 1) * BR
LIMIT = 16 * 1024 * 1024
LARGE = 56 * 1024 * 1024
WIDTH = 2 * HALF + 128
TILES = 3 * HALF // 128
ROWS = SLOTS * TILES


def iota(shape, dim):
    return lax.broadcasted_iota(I32, shape, dim)


def onehot(mask):
    return jnp.where(mask, 1.0, 0.0).astype(BF)


def dot(a, b):
    return jnp.dot(a, b, preferred_element_type=F32)


def dot_nt(a, b):
    return lax.dot_general(a, b, (((1,), (1,)), ((), ())), preferred_element_type=F32)


VMEM, HBM, ANY, SMEM = pltpu.VMEM, pltpu.HBM, pl.ANY, pltpu.SMEM


def call(kernel, outs, args, scalars=0, scratch=(), flops=0, moved=0, outside=(), space=ANY, limit=LIMIT):
    specs = [
        pl.BlockSpec(memory_space=SMEM if i < scalars else space if i in outside else VMEM)
        for i in range(len(args))
    ]
    return pl.pallas_call(
        kernel,
        out_shape=[jax.ShapeDtypeStruct(s, d) for s, d in outs],
        in_specs=specs,
        out_specs=[pl.BlockSpec(memory_space=VMEM)] * len(outs),
        scratch_shapes=list(scratch),
        compiler_params=pltpu.CompilerParams(vmem_limit_bytes=limit),
        cost_estimate=pl.CostEstimate(flops=flops, bytes_accessed=moved, transcendentals=0),
    )(*args)


def pieces_of(value):
    high = value.astype(BF).astype(F32)
    mid = (value - high).astype(BF).astype(F32)
    return high, mid, value - high - mid


def pack_kernel(place, x_in, up_in, w_in, bias_in, owner_in, top_ref, bottom_ref, out_ref, x_ref, up_ref, bias_ref, owner_ref, rows, ups, sems):
    copies = [
        pltpu.make_async_copy(source, target, sems.at[i])
        for i, (source, target) in enumerate(
            [
                (up_in, up_ref),
                (x_in, x_ref),
                (bias_in, bias_ref),
                (owner_in, owner_ref),
                (w_in.at[pl.ds(0, SHARE), :], top_ref.at[pl.ds(SIDE, SHARE), :]),
                (w_in.at[pl.ds(SHARE, SHARE), :], bottom_ref),
            ]
        )
    ]
    for copy in copies:
        copy.start()
    skip = place[0] % 2 * 64
    k, lane = iota((256, 384), 0) - skip, iota((256, 384), 1)
    pick = (lane < 128) & (k == lane)
    pick = pick | ((lane >= 128) & (lane < 192) & (k == lane))
    pick = onehot(pick | ((lane >= 320) & (k == lane - 192)))
    k, lane = iota((RHO, RHO), 0), iota((RHO, RHO), 1)
    block = k // 16 == lane // 16
    k, lane = k % 16, lane % 16
    kept = onehot(block & (k == lane) & (k < SLOTS))
    kept_even = onehot(block & (lane == 2 * (k - SLOTS)))
    kept_odd = onehot(block & (lane == 2 * (k - SLOTS) + 1))
    r, c = iota((16, 16), 0), iota((16, 16), 1)
    same = onehot((r == c) & (r < SLOTS))
    even = onehot(c == 2 * (r - SLOTS))
    odd = onehot(c == 2 * (r - SLOTS) + 1)
    rows[...] = jnp.zeros_like(rows)
    ups[...] = jnp.zeros_like(ups)
    copies[0].wait()
    for z in range(NZ):
        start = pl.multiple_of(z * GROUP + place[0] * 3 // 2 * 128, 128)
        ups[z * 16 : z * 16 + SLOTS, :] = up_ref[:, pl.ds(start, 256)]
    chosen = dot(ups[...], pick).astype(BF)
    chosen = dot(kept, chosen[:, :128]) + dot(kept_even, chosen[:, 128:256]) + dot(kept_odd, chosen[:, 256:])
    chosen = chosen.astype(BF)
    copies[1].wait()
    rows[0:SLOTS, :] = x_ref[...]
    a, b, last = rows[:, :HALF], rows[:, HALF : 2 * HALF], rows[:, 2 * HALF :]
    left = (dot(same, a) + dot(even, last)).astype(BF)
    right = (dot(same, b) + dot(odd, last)).astype(BF)
    for z in range(NZ):
        out_ref[z, :, :HALF] = left
        out_ref[z, :, HALF : 2 * HALF] = right
        out_ref[z, :, 2 * HALF :] = chosen[z * 16 : z * 16 + 16]
    copies[2].wait()
    row = iota((SIDE, HID), 0)
    high, mid, low = pieces_of(bias_ref[...].reshape(1, HID))
    side = jnp.where(row == 1, high, jnp.where(row == 2, mid, jnp.where(row == 3, low, 0.0)))
    copies[3].wait()
    owner = jnp.where(iota((SIDE, DP), 0) == 0, owner_ref[...].astype(F32), 0.0).astype(BF)
    owner = dot(owner, onehot(iota((DP, HID), 0) == iota((DP, HID), 1)))
    top_ref[:SIDE, :HID] = (owner + side).astype(BF)
    top_ref[:SIDE, HID:] = jnp.zeros((SIDE, 3 * HALF - HID), BF)
    copies[4].wait()
    copies[5].wait()


def sum_rows(total):
    high, mid, low = pieces_of(total)
    lane = iota((SHARE, 128), 1)
    pieces = jnp.where(lane == 0, high, jnp.where(lane == 1, mid, jnp.where(lane == 2, low, 0.0)))
    pieces = jnp.concatenate([pieces, jnp.zeros((256 - SHARE, 128), F32)], axis=0).T[:16].astype(BF)
    r, c = iota((16, 16), 0), iota((16, 16), 1)
    shift = onehot(iota((128, 128), 0) + 64 == iota((128, 128), 1))
    rest = dot(pieces[:, 128:], shift).astype(BF)
    head = (c < 3) & (r == jnp.where(c < 2, c + 6, 14))
    rows = dot(onehot(head), pieces[:, :128]) + dot(onehot((r == c + 8) & (c < 3)), rest)
    return rows.astype(BF)


def slot_of(i):
    tail = (i - MAIN) % TAIL
    return jnp.where(i < MAIN, i // 8, tail // 2), jnp.where(i < MAIN, i % 8, 8 + tail % 2)


def selector(third):
    i, rho = iota((256, RHO), 0), iota((256, RHO), 1)
    z, slot = slot_of(i)
    if third == 0:
        return onehot(rho == z * 16 + slot)
    return onehot((rho == z * 16 + SLOTS + slot // 2) & (slot % 2 == third - 1))


def by_quarter(pieces):
    lane = iota((QUARTER, 128), 1) // 32
    found = jnp.where(lane == 0, pieces[0], 0.0)
    for g in range(1, 4):
        found = jnp.where(lane == g, pieces[g], found)
    return found


def select_rows(rz_ref, x_ref, column_ref):
    left, right = rz_ref[:, :HALF], rz_ref[:, HALF : 2 * HALF]
    first = selector(0)
    x_ref[:, :HALF] = dot(first, left).astype(BF)
    x_ref[:, HALF : 2 * HALF] = dot(first, right).astype(BF)
    x_ref[:, 2 * HALF :] = (dot(selector(1), left) + dot(selector(2), right)).astype(BF)
    column_ref[...] = x_ref[: MAIN + TAIL, :]


def ups_kernel(rz_ref, ug_ref, held):
    ups = rz_ref[:, 2 * HALF :]
    r, c = iota((128, 128), 0), iota((128, 128), 1)
    low, high = dot(ups, onehot((r == c) & (r < 64))).astype(BF), dot(ups, onehot(r == c + 64)).astype(BF)
    for part, rest in (
        (dot(selector(0), ups), slice(0, 128)),
        (dot(selector(1), low) + dot(selector(2), high), slice(128, SHARE)),
    ):
        main, tail = part[:MAIN].T, part[MAIN:].T
        held[rest, :MAIN] = main[: rest.stop - rest.start]
        held[rest, MAIN:] = tail[: rest.stop - rest.start]
    ug_ref[:SHARE, :] = held[:, :MAIN]
    ug_ref[SHARE:, :] = by_quarter([held[g * QUARTER : (g + 1) * QUARTER, MAIN:] for g in range(4)])


def partial(piece, start, x, out):
    found = dot_nt(piece[start : start + SHARE, :], x)
    out[:SHARE, :] = found[:, :MAIN].astype(BF)
    tail = [found[g * QUARTER : (g + 1) * QUARTER, MAIN:] for g in range(4)]
    out[SHARE:, :] = by_quarter(tail).astype(BF)


def near_kernel(rz_ref, *refs):
    pieces, (x_ref, column_ref, out_ref, side_ref) = refs[:6], refs[6:]
    select_rows(rz_ref, x_ref, column_ref)
    x = x_ref[...]
    for n, piece in enumerate(pieces):
        partial(piece, SIDE if n % 2 == 0 else 0, x, out_ref.at[n])
        if n % 2 == 0:
            side_ref[n // 2] = piece[:SIDE, :HID]


def pre_kernel(place, x_ref, near_ref, near_side, top_ref, bottom_ref, out_ref, side_ref):
    x = x_ref[...]
    far = (place[1] + 2) % NX
    partial(top_ref, SIDE, x, out_ref.at[2 * far])
    partial(bottom_ref, 0, x, out_ref.at[2 * far + 1])
    side_ref[far] = top_ref[:SIDE, :HID].astype(F32)
    for n, step in enumerate((0, 1, 3)):
        source = (place[1] + step) % NX
        out_ref[2 * source] = near_ref[2 * n]
        out_ref[2 * source + 1] = near_ref[2 * n + 1]
        side_ref[source] = near_side[n].astype(F32)


def gelu_slope(values):
    inner_arg = 0.7978845608 * (values + 0.044715 * values * values * values)
    tangent = jnp.tanh(inner_arg)
    return 0.5 * (1.0 + tangent) + 0.5 * values * (1.0 - tangent * tangent) * 0.7978845608 * (
        1.0 + 3.0 * 0.044715 * values * values
    )


def grad_kernel(place, parts_ref, ug_ref, side_ref, counts_ref, out_ref, sums_ref):
    tensor, x_me = place[0], place[1]
    side = side_ref[tensor // 2]
    bias = side[1:2] + side[2:3] + side[3:4]
    wanted = iota((SHARE, HID), 1) == (tensor % 2) * SHARE + iota((SHARE, HID), 0)
    bias = jnp.sum(jnp.where(wanted, bias, 0.0), axis=1, keepdims=True)
    counts = jnp.broadcast_to(counts_ref[...].astype(F32), (8, DP)).astype(BF)
    s = iota((DP, 128), 0)
    lane = iota((DP, 128), 1)
    many = dot(counts, onehot(s == lane // 8 * NX + x_me))[0:1]
    few = dot(counts, onehot(s == lane % TAIL // 2 * NX + x_me))[0:1]
    lane = iota((1, 128), 1)
    many = (lane % 8).astype(F32) < many
    few = (8 + lane % 2).astype(F32) < few
    pre = parts_ref[0].astype(F32)
    for j in range(1, NT):
        pre = pre + parts_ref[j].astype(F32)
    tail_bias = by_quarter([bias[g * QUARTER : (g + 1) * QUARTER] for g in range(4)])
    main = jnp.where(many, ug_ref[:SHARE] * gelu_slope(pre[:SHARE] + bias), 0.0)
    tail = jnp.where(few, ug_ref[SHARE:] * gelu_slope(pre[SHARE:] + tail_bias), 0.0)
    out_ref[:SHARE, :] = main.astype(BF)
    out_ref[SHARE:PACK, :] = tail.astype(BF)
    lane = iota((QUARTER, 128), 1) // 32
    total = jnp.sum(main, axis=1, keepdims=True) + jnp.concatenate(
        [jnp.sum(jnp.where(lane == g, tail, 0.0), axis=1, keepdims=True) for g in range(4)], axis=0
    )
    sums_ref[...] = sum_rows(total)


def unpacked(tail):
    lane = iota((QUARTER, 128), 1) // 32
    zero = jnp.zeros((), BF)
    return jnp.concatenate([jnp.where(lane == g, tail, zero) for g in range(4)], axis=0)


def moved_kernel(place, low_ref, other_ref, sums_ref, side_ref, out_ref):
    tensor, x_me = place[0], place[1]
    m = tensor % 2
    blocks = HID // BR
    owner = side_ref[tensor // 2][0:1, :blocks]
    r, c = iota((blocks, blocks), 0), iota((blocks, blocks), 1)
    column = jnp.sum(jnp.where(r == c, owner, 0.0), axis=1, keepdims=True)
    rank = jnp.sum(jnp.where((column == owner) & (r < c), 1.0, 0.0), axis=0, keepdims=True)
    target = jnp.broadcast_to(owner * MOST + rank, (8, blocks)).astype(BF)
    block, unit = iota((blocks, HID), 0), iota((blocks, HID), 1)
    within = unit - block * BR
    member = (within >= 0) & (within < BR)
    offset = jnp.sum(jnp.where(member, within, 0).astype(F32), axis=0, keepdims=True)
    key = dot(target, onehot(member))[0:1] * BR + offset
    low, other = low_ref[...], other_ref[...]
    both = [jnp.where(m == 0, low, other), jnp.where(m == 0, other, low)]
    main = jnp.concatenate([g[:SHARE] for g in both], axis=0)
    tail = jnp.concatenate([unpacked(g[SHARE:PACK]) for g in both], axis=0)
    r, c = iota((128, 128), 0), iota((128, 128), 1)
    tail = dot(tail, onehot((r % TAIL == c) & (c < TAIL))).astype(BF)
    rho = iota((DP * 8, 1), 0)
    dest, row = rho // 8, rho % 8
    wanted = (dest * MOST + m) * BR + row
    wanted = jnp.where(row < BR, wanted, -1).astype(F32)
    found = dot(onehot(wanted == key), jnp.concatenate([main, tail], axis=1))
    sums = sums_ref[...].astype(F32)
    for e in range(DP):
        here = found[e * 8 : (e + 1) * 8]
        here = jnp.concatenate([here[:, :128], here[:, 128:]], axis=0) + sums
        out_ref[e * 16 : (e + 1) * 16, :] = here.astype(BF)


def out_kernel(place, g_ref, *refs):
    pieces, (px_ref, full) = refs[: 2 * NX], refs[2 * NX :]
    for n in range(2 * NX):
        j = (place[1] + n // 2) % NX * 2 + n % 2
        full[n * SHARE : (n + 1) * SHARE, :MAIN] = g_ref[j, :SHARE, :]
        full[n * SHARE : (n + 1) * SHARE, MAIN:] = unpacked(g_ref[j, SHARE:PACK, :])
    g = full[...]
    rho, lane = iota((2 * MAIN, 256), 0), iota((2 * MAIN, 256), 1)
    tail = (lane >= MAIN) & (lane % TAIL == (rho - MAIN) // 4)
    tail = tail & (rho >= MAIN)
    here = dot_nt(onehot(tail | ((lane == rho) & (rho < MAIN))), g).astype(BF)
    total = jnp.zeros((2 * MAIN, 3 * HALF), F32)
    for n, piece in enumerate(pieces):
        start = SIDE if n % 2 == 0 else 0
        total = total + dot(here[:, n * SHARE : (n + 1) * SHARE], piece[start:, :])
    tiles = [total[:MAIN, t * 128 : (t + 1) * 128] for t in range(TILES)]
    quarter = iota((MAIN, 128), 0) % 4
    for i in range(TILES // 4):
        tile = jnp.zeros((MAIN, 128), F32)
        for q in range(4):
            t = 4 * i + q
            tile = jnp.where(quarter == q, total[MAIN:, t * 128 : (t + 1) * 128], tile)
        tiles.append(tile)
    for z in range(NZ):
        blocks = [tile[z * 8 : (z + 1) * 8] for tile in tiles]
        for u in range(len(blocks) // 2):
            both = jnp.concatenate([blocks[2 * u], blocks[2 * u + 1]], axis=0)
            px_ref[z, u * 16 : (u + 1) * 16, :] = both.astype(BF)
        px_ref[z, ROWS - 8 :, :] = blocks[-1].astype(BF)


def order_kernel(place, weights_there, columns_there, in_ref, out_ref, block):
    del weights_there, columns_there
    n = BR * NZ
    r, c = iota((2 * n, RHO), 0), iota((2 * n, RHO), 1)
    row = r // NZ
    pick = onehot((c // 16 == r % NZ) & (c % 16 == jnp.where(row < BR, row, row + 8 - BR)))
    r, c = iota((128, 128), 0), iota((128, 128), 1)
    tail = jnp.zeros((n, 128), F32)
    sums = jnp.zeros((16, 128), F32)
    for x in range(NX):
        for z in range(NZ):
            block[z * 16 : (z + 1) * 16, :] = in_ref[z * NX + x]
        found = dot(pick, block[...]).astype(BF)
        out_ref[x * n : (x + 1) * n, :] = found[:n]
        tail = tail + dot(found[n:], onehot((r < TAIL) & (c == r + x * TAIL)))
        sums = sums + in_ref[place[2] * NX + x].astype(F32)
    out_ref[NX * n : MOVED * NZ, :] = tail.astype(BF)
    row = iota((8, 128), 0)
    for i, (a, b, c) in enumerate(((6, 7, 14), (8, 9, 10))):
        total = sums[c : c + 1] + sums[b : b + 1] + sums[a : a + 1]
        high, mid, low = pieces_of(total)
        part = jnp.where(row == 0, high, jnp.where(row == 1, mid, jnp.where(row == 2, low, 0.0)))
        parts = part if i == 0 else jnp.concatenate([parts, part], axis=0)
    out_ref[MOVED * NZ :, :] = parts.astype(BF)


def slots_kernel(in_ref, out_ref, held):
    total = in_ref[0].astype(F32)
    for z in range(1, NZ):
        total = total + in_ref[z].astype(F32)
    for t in range(TILES):
        span = slice(t * 128, (t + 1) * 128)
        held[:8, span] = total[t * 8 : (t + 1) * 8]
        for s in range(2):
            row = 8 * TILES + t // 4 * 8 + s * 4 + t % 4
            held[8 + s : 9 + s, span] = total[row : row + 1]
    out_ref[...] = held[:SLOTS, :].astype(BF)


def weight_kernel(place, m_ref, *refs):
    columns, (out_ref, bias_ref, found, held) = refs[:NX], refs[NX:]
    lane, unit = iota((128, HID), 0), iota((128, HID), 1)
    row = iota((16, 128), 0)
    total = jnp.zeros((16, HID), F32)
    for h in range(2):
        sums = m_ref[place[1] * 2 + h, MOVED * NZ :, :]
        for i in range(2):
            mine = (unit == h * SHARE + i * 64 + lane) & (lane >= i * 64)
            total = total + dot(jnp.where(row // 8 == i, sums, jnp.zeros((), BF)), onehot(mine))
    total = total[:8] + total[8:]
    bias_ref[...] = (total[2:3] + total[1:2] + total[0:1]).reshape(HID)
    n = BR * NZ
    for j in range(NT):
        for k in range(NX + 1):
            start = pl.multiple_of((place[1] + k) % NX * n, n) if k < NX else NX * n
            block = m_ref[j, pl.ds(start, n), :]
            for b in range(BR):
                row = b * MOST * DP + j * NZ
                found[row : row + NZ, k * 128 : (k + 1) * 128] = block[b * NZ : (b + 1) * NZ]
    r, c = iota((MOST * DP, MOST * DP), 0), iota((MOST * DP, MOST * DP), 1)
    order = onehot(c == r % NT * NZ + r // NT)
    for k, column in enumerate(columns):
        held[k * MAIN : (k + 1) * MAIN, :] = column[:MAIN, :]
        start = pl.multiple_of(NX * MAIN + (place[1] + k) % NX * TAIL, TAIL)
        held[pl.ds(start, TAIL), :] = column[MAIN:, :]
    for b in range(BR):
        span = slice(b * MOST * DP, (b + 1) * MOST * DP)
        found[span, :] = dot(order, found[span, :]).astype(BF)
    for third in range(3):
        span = slice(third * HALF, (third + 1) * HALF)
        total = dot(found[...], held[:, span]).astype(BF)
        for b in range(BR):
            out_ref[b, :, span] = total[b * MOST * DP : (b + 1) * MOST * DP]


def arrived_kernel(*refs):
    refs[-1][0] = 0


def arrived(arrays):
    return pl.pallas_call(
        arrived_kernel,
        out_shape=jax.ShapeDtypeStruct((1,), I32),
        in_specs=[pl.BlockSpec(memory_space=ANY)] * len(arrays),
        out_specs=pl.BlockSpec(memory_space=SMEM),
        cost_estimate=pl.CostEstimate(flops=50 * 10**9, bytes_accessed=0, transcendentals=0),
    )(*arrays)


def to_left(value):
    return lax.ppermute(value, "x", [(i, (i - 1) % NX) for i in range(NX)])


def to_right(value):
    return lax.ppermute(value, "x", [(i, (i + 1) % NX) for i in range(NX)])


def across(value):
    return lax.ppermute(value, "x", [(i, (i + 2) % NX) for i in range(NX)])


def body(x_slots, counts, w, bias, upstream, owners):
    tensor = lax.axis_index(("y", "core")).astype(I32)
    x_me = lax.axis_index("x").astype(I32)
    place = jnp.stack([tensor, x_me, lax.axis_index("z").astype(I32)])
    top, bottom, packed = call(
        pack_kernel,
        [((FIRST, 3 * HALF), BF), ((SHARE, 3 * HALF), BF), ((NZ, 16, WIDTH), BF)],
        [place, x_slots, upstream, w, bias, owners.reshape(1, DP)],
        1,
        [
            VMEM((SLOTS, 3 * HALF), BF),
            VMEM((SLOTS, NZ * GROUP), BF),
            VMEM((HID,), F32),
            VMEM((1, DP), I32),
            VMEM((16, 3 * HALF), BF),
            VMEM((RHO, 256), BF),
            pltpu.SemaphoreType.DMA((6,)),
        ],
        2 * RHO * GROUP * 256,
        5 * 10**6,
        (1, 2, 3, 4, 5),
        HBM,
        LARGE,
    )
    next_top, prev_bottom = to_left(top), to_right(bottom)
    along_z = lax.all_to_all(packed, "z", 0, 0, tiled=True)
    there = arrived([next_top, prev_bottom])
    top, bottom, next_top, prev_bottom, there = lax.optimization_barrier((top, bottom, next_top, prev_bottom, there))
    far_top, far_bottom = to_left(next_top), to_right(prev_bottom)
    next_bottom, prev_top = to_left(bottom), to_right(top)
    pieces = [top, bottom, next_top, next_bottom, far_top, far_bottom, prev_top, prev_bottom]
    rows, column, near, near_side = call(
        near_kernel,
        [((256, 3 * HALF), BF), ((MAIN + TAIL, 3 * HALF), BF), ((6, PACK, 128), BF), ((3, SIDE, HID), BF)],
        [along_z.reshape(RHO, WIDTH)] + pieces[:4] + pieces[6:],
        flops=2 * GROUP * 256 * 3 * HALF,
        moved=4 * 10**6,
    )
    part, side = call(
        pre_kernel,
        [((NT, PACK, 128), BF), ((NX, SIDE, HID), F32)],
        [place, rows, near, near_side] + pieces[4:6],
        1,
        flops=GROUP * 256 * HALF,
        moved=2 * 10**6,
    )
    part, along_z = lax.optimization_barrier((part, along_z))
    ug, = call(
        ups_kernel,
        [((PACK, 128), F32)],
        [along_z.reshape(RHO, WIDTH)],
        0,
        [VMEM((SHARE, 256), F32)],
        flops=10**9,
        moved=10**6,
    )
    columns = [column, to_left(column), across(column), to_right(column)]
    columns_there = arrived(columns[1::2])
    parts = lax.all_to_all(part, ("y", "core"), 0, 0, tiled=True)
    low, sums = call(
        grad_kernel,
        [((PACK, 128), BF), ((16, 128), BF)],
        [place, parts, ug, side, counts.reshape(1, DP)],
        1,
        moved=10**6,
    )
    other = lax.ppermute(low, "core", [(0, 1), (1, 0)])
    sent, = call(
        moved_kernel,
        [((DP * 16, 128), BF)],
        [place, low, other, sums, side],
        1,
        flops=2 * 8 * 96 * HID * 128,
        moved=10**6,
    )
    moved = lax.all_to_all(sent.reshape(DP, 16, 128), ("z", "x"), 0, 0, tiled=True)
    low, sent = lax.optimization_barrier((low, sent))
    grad = lax.all_gather(low, ("y", "core"), axis=0)
    px, = call(
        out_kernel,
        [((NZ, ROWS, 128), BF)],
        [place, grad] + pieces,
        1,
        [VMEM((GROUP, 256), BF)],
        2 * RHO * GROUP * (4 * HALF + 3 * 256),
        6 * 10**6,
    )
    px, moved, columns_there = lax.optimization_barrier((px, moved, columns_there))
    pz = lax.all_to_all(px, "z", 0, 0, tiled=True)
    moved, = call(
        order_kernel,
        [((MOVED * NZ + 16, 128), BF)],
        [place, there, columns_there, moved],
        3,
        [VMEM((RHO, 128), BF)],
        moved=10**6,
    )
    moved = lax.all_gather(moved, ("y", "core"), axis=0)
    found, grad_bias = call(
        weight_kernel,
        [((BR, MOST * DP, 3 * HALF), BF), ((HID,), F32)],
        [place, moved] + columns,
        1,
        [VMEM((NT * BR * NZ, 640), BF), VMEM((NX * (MAIN + TAIL), 3 * HALF), BF)],
        2 * 768 * 640 * 1536,
        5 * 10**6,
    )
    grad_slots, = call(
        slots_kernel, [((SLOTS, 3 * HALF), BF)], [pz], 0, [VMEM((16, 3 * HALF), F32)], moved=10**6
    )
    return grad_slots, grad_bias, found.transpose(1, 0, 2)


def solution(mesh):
    fine = Mesh(mesh.devices.reshape(NZ, NX, NT // 2, 2), ("z", "x", "y", "core"))
    rows, cols = ("z", "x"), ("y", "core")
    in_specs = (P(rows, cols), P(), P(rows, cols), P(rows), P(rows, None), P(rows, None))
    out_specs = (P(rows, cols), P(rows), P(rows, None, cols))
    return jax.shard_map(body, mesh=fine, in_specs=in_specs, out_specs=out_specs, check_vma=False)
```
